256 devices in a mesh: ctx: 32 (over y, x, core), tp: 8 (over z).
Axes of the slice: x: 4, y: 4, z: 8, core: 2. Of those that a mesh axis runs over, the one named last changes fastest.
Arguments:
- query: bfloat16 [8192, 4096], P('ctx', 'tp'), may hold values from -6 to 6
- keys: bfloat16 [8192, 4096], P('ctx', 'tp'), may hold values from -6 to 6
- values: bfloat16 [8192, 4096], P('ctx', 'tp'), may hold values from -6 to 6
- filt: float32 [8192, 4096], P('ctx', 'tp'), may hold values from -1 to 1
- direct: float32 [4096], P('tp'), may hold values from -4 to 4
- w_out: bfloat16 [4096, 4096], P('tp'), may hold values from -0.09375 to 0.09375
Outputs:
- output: bfloat16 [8192, 4096], P('ctx', 'tp')
The draws below stay inside these ranges and needn't reach their ends.
All inputs are finite; a program needn't handle non-finite values.
Results may differ from the reference program's by a relative error of at most 0.0049.
Values sent between devices are 32-bit elements; how exact they have to be, the bound alone decides.
A program may use at most 128 MiB of HBM per device.

```python
import math
import jax
import jax.numpy as jnp
from jax import lax

D = 4096
TOKENS = 8192


def draw_filt(key, part):
    key = jax.random.fold_in(key, 7)
    key_rate = jax.random.fold_in(key, 1)
    key_taps = jax.random.fold_in(key, 2)
    key_floor = jax.random.fold_in(key, 3)
    low = math.log(30.0)
    high = math.log(4.0 * TOKENS)
    total = float(TOKENS)
    reach = jnp.exp(jax.random.uniform(key_rate, (D,), jnp.float32, low, high))
    floor_level = jnp.sqrt(jax.random.uniform(key_floor, (D,), jnp.float32, 10.0, 40.0) / total)
    places = jnp.arange(TOKENS, dtype=jnp.float32)[:, None]
    envelope = jnp.exp(-places / reach[None, :]) + floor_level[None, :]
    first_sum = jnp.expm1(-total / reach) / jnp.expm1(-1.0 / reach)
    second_sum = jnp.expm1(-2.0 * total / reach) / jnp.expm1(-2.0 / reach)
    energy = second_sum + 2.0 * floor_level * first_sum + floor_level * floor_level * total
    scale = 0.6 / jnp.sqrt(energy)
    taps = jnp.clip(jax.random.normal(key_taps, (TOKENS, D), jnp.float32), -6.0, 6.0)
    return (taps * envelope * scale[None, :]).astype(jnp.float32)


def block_scale(own_key, dims, shards, least, top_value):
    def one(dim, blocks):
        heights = jax.random.uniform(jax.random.fold_in(jax.random.fold_in(own_key, 6), dim), (blocks,), jnp.float32, least / len(shards), top_value / len(shards))
        return jnp.repeat(jnp.exp(heights), dims[dim] // blocks).reshape((-1,) + (1,) * (len(dims) - dim - 1))

    gain = one(*shards[0])
    for cut in shards[1:]:
        gain = gain * one(*cut)
    return gain


def noise(stream_key, shape, width, limit, shards=(), kind=jnp.bfloat16):
    entries = jax.random.normal(stream_key, shape, jnp.float32) * width
    if len(shards) > 0:
        entries = block_scale(stream_key, shape, shards, -0.22, 0.18) * entries
    return jnp.clip(entries, min=-limit, max=limit).astype(kind)


def setup_inputs(seed: int = 0) -> dict:
    key_list = jax.random.split(jax.random.key(seed), 7)
    return {
        "query": noise(key_list[0], (TOKENS, D), 1.0, 6.0, ((0, 32), (1, 8))),
        "keys": noise(key_list[1], (TOKENS, D), 1.0, 6.0, ((0, 32), (1, 8))),
        "values": noise(key_list[2], (TOKENS, D), 1.0, 6.0, ((0, 32), (1, 8))),
        "filt": draw_filt(jax.random.fold_in(key_list[6], 71), 0),
        "direct": noise(key_list[4], (D,), 0.3, 4.0, ((0, 8),), jnp.float32),
        "w_out": noise(key_list[5], (D, D), D ** -0.5, 0.09375, ((0, 8),)),
    }


def reference(query, keys, values, filt, direct, w_out):
    signal = keys.astype(jnp.float32) * values.astype(jnp.float32)
    block = math.gcd(D, 256)
    count = D // block
    sig_blocks = signal.T.reshape(count, block, TOKENS)
    flt_blocks = filt.T.reshape(count, block, TOKENS)

    def convolve(pair):
        spec = jnp.fft.rfft(pair[0], n=2 * TOKENS, axis=-1) * jnp.fft.rfft(pair[1], n=2 * TOKENS, axis=-1)
        return jnp.fft.irfft(spec, n=2 * TOKENS, axis=-1)[:, :TOKENS]

    conv = lax.map(convolve, (sig_blocks, flt_blocks)).reshape(D, TOKENS).T.astype(jnp.float32)
    gated = (query.astype(jnp.float32) * (conv + direct[None, :] * signal)).astype(jnp.bfloat16)
    return jnp.dot(gated, w_out, preferred_element_type=jnp.float32).astype(jnp.bfloat16)
```

```python
import functools
import math

import jax
import jax.numpy as jnp
import numpy as np
from jax import lax
from jax.experimental import pallas as pl
from jax.experimental.pallas import tpu as pltpu
from jax.sharding import PartitionSpec as P

MESH = pl.DeviceIdType.MESH
F32 = jnp.float32
BF16 = jnp.bfloat16
LANES = 128
SUB = 8
CHUNKS = 2


def tables(block):
    order = np.concatenate([np.arange(0, block, 2), np.arange(1, block, 2)])
    place = np.arange(block)
    angle = math.pi * (2 * order[None, :] + 1) * place[:, None] / (2 * block)
    forward = np.concatenate([np.cos(angle), -np.sin(angle)], axis=1)
    inverse = np.concatenate([np.cos(angle.T), -np.sin(angle.T)], axis=0) / block
    out = []
    for table in (forward, inverse):
        high = table.astype(jnp.bfloat16)
        low = (table - high.astype(np.float64)).astype(jnp.bfloat16)
        out += [high, low]
    return out


def split(x):
    high = x.astype(BF16)
    return high, (x - high.astype(F32)).astype(BF16)


def dot3(x, high, low):
    xh, xl = split(x)
    total = jnp.dot(xh, low, preferred_element_type=F32)
    total += jnp.dot(xl, high, preferred_element_type=F32)
    return total + jnp.dot(xh, high, preferred_element_type=F32)


def kernel(
    nc, nz,
    q_hbm, k_hbm, v_hbm, f_hbm, d_hbm, w_hbm, th_hbm, tl_hbm, ih_hbm, il_hbm,
    o_ref,
    q, k, v, f, dr, w, th, tl, ih, il,
    sbuf, rbuf, sb, gb, zb, yb, cb, gated, snd, rcv,
    lsem, asend, arecv, bsend, brecv, zsend, zrecv,
):
    c = lax.axis_index("ctx")
    z = lax.axis_index("tp")
    block, chans = k.shape
    groups = sbuf.shape[0]
    width = groups * SUB

    loads = [
        pltpu.make_async_copy(src, dst, lsem.at[n])
        for n, (src, dst) in enumerate(
            [(k_hbm, k), (v_hbm, v), (f_hbm, f), (q_hbm, q), (d_hbm, dr), (th_hbm, th),
             (tl_hbm, tl), (ih_hbm, ih), (il_hbm, il), (w_hbm, w)]
        )
    ]
    for load in loads:
        load.start()

    barrier = pltpu.get_barrier_semaphore()

    def greet(d, _):
        pl.semaphore_signal(
            barrier, inc=1, device_id=(lax.rem(c + d, nc), z), device_id_type=MESH
        )
        return 0

    lax.fori_loop(1, nc, greet, 0)
    right, left = lax.rem(z + 1, nz), lax.rem(z + nz - 1, nz)
    for other in (right, left):
        pl.semaphore_signal(barrier, inc=1, device_id=(c, other), device_id_type=MESH)

    loads[0].wait()
    loads[1].wait()
    loads[2].wait()
    per = LANES // width
    for j in range(chans // LANES):
        cols = slice(j * LANES, (j + 1) * LANES)
        for which in range(2):
            if which == 0:
                part = k[:, cols].astype(F32) * v[:, cols].astype(F32)
            else:
                part = f[:, cols]
            part = part.T.reshape(per, groups, SUB, block)
            for g in range(groups):
                sbuf[g, which, j * per:(j + 1) * per] = part[:, g]
    for g in range(groups):
        rbuf[g, :, c] = sbuf[g, :, c]

    pl.semaphore_wait(barrier, nc + 1)

    def to_owner(g, d):
        t = lax.rem(c + d, nc)
        return pltpu.make_async_remote_copy(
            sbuf.at[g, :, t], rbuf.at[g, :, c], asend.at[g, d], arecv.at[g, d],
            device_id=(t, z), device_id_type=MESH,
        )

    def to_place(g, d):
        t = lax.rem(c + d, nc)
        rows = pl.ds(pl.multiple_of(c * width + g * SUB, SUB), SUB)
        return pltpu.make_async_remote_copy(
            yb.at[g, t], cb.at[rows], bsend.at[g, d], brecv.at[g, d],
            device_id=(t, z), device_id_type=MESH,
        )

    def each(make, act, g):
        def step(d, _):
            getattr(make(g, d), act)()
            return 0

        lax.fori_loop(1, nc, step, 0)

    for g in range(groups):
        each(to_owner, "start", g)
    for load in loads[3:]:
        load.wait()

    half = block // 2
    gb[:, :, 0:SUB] = jnp.zeros((2, 2, SUB, SUB, LANES), F32)
    for g in range(groups):
        each(to_owner, "wait_recv", g)
        flat = (nc * SUB, block)
        spec = dot3(rbuf[g, 0].reshape(flat), th[...], tl[...])
        for part in range(2):
            for tile in range(2):
                at = part * block + tile * half
                sb[tile, part] = spec[:, at:at + half].reshape(nc, SUB, LANES)
        spec = dot3(rbuf[g, 1].reshape(flat), th[...], tl[...])
        zero = jnp.zeros((1, SUB, LANES), F32)
        for tile in range(2):
            at = tile * half
            real = spec[:, at:at + half].reshape(nc, SUB, LANES)
            imag = spec[:, block + at:block + at + half].reshape(nc, SUB, LANES)
            real_b = jnp.concatenate([zero, real[:-1]], axis=0)
            imag_b = jnp.concatenate([zero, imag[:-1]], axis=0)
            if tile == 0:
                real, imag = real - imag_b, imag + real_b
            else:
                real, imag = real + imag_b, imag - real_b
            gb[tile, 0, SUB:] = real
            gb[tile, 1, SUB:] = imag

        def combine(tile, _):
            for hi in range(nc // SUB):
                acc_r = [None] * SUB
                acc_i = [None] * SUB
                for lo in range(hi + 1):
                    srcs = [(sb[tile, 0, lo * SUB + n], sb[tile, 1, lo * SUB + n]) for n in range(SUB)]
                    base = (hi - lo) * SUB
                    for diff in range(1 - SUB, SUB):
                        if base + diff < 0:
                            continue
                        fr = gb[tile, 0, SUB + base + diff]
                        fi = gb[tile, 1, SUB + base + diff]
                        for n in range(SUB):
                            a = n + diff
                            if a < 0 or a >= SUB:
                                continue
                            sr, si = srcs[n]
                            pr = sr * fr - si * fi
                            pi = sr * fi + si * fr
                            acc_r[a] = pr if acc_r[a] is None else acc_r[a] + pr
                            acc_i[a] = pi if acc_i[a] is None else acc_i[a] + pi
                for a in range(SUB):
                    zb[0, tile, hi * SUB + a] = acc_r[a]
                    zb[1, tile, hi * SUB + a] = acc_i[a]
            return 0

        lax.fori_loop(0, 2, combine, 0)
        whole = jnp.concatenate(
            [zb[p, t].reshape(nc * SUB, LANES) for p in range(2) for t in range(2)], axis=1
        )
        yb[g] = dot3(whole, ih[...], il[...]).reshape(nc, SUB, block)
        rows = pl.ds(pl.multiple_of(c * width + g * SUB, SUB), SUB)
        cb[rows] = yb[g, c]
        each(to_place, "start", g)
    for g in range(groups):
        each(to_place, "wait_recv", g)

    for j in range(chans // LANES):
        cols = slice(j * LANES, (j + 1) * LANES)
        signal = k[:, cols].astype(F32) * v[:, cols].astype(F32)
        conv = cb[cols, :].T
        gate = q[:, cols].astype(F32) * (conv + dr[:, cols] * signal)
        gated[:, cols] = gate.astype(BF16)

    out_cols = o_ref.shape[1]
    span = block // 2
    rows_of = span // CHUNKS

    def dest(way, s):
        step = nz - 1 - s if way == 0 else 1 + s
        return lax.rem(z + step, nz)

    def local(way, s):
        cols = pl.ds(pl.multiple_of(dest(way, s) * out_cols, out_cols), out_cols)
        return jnp.dot(
            gated[way * span:(way + 1) * span, :], w[:, cols], preferred_element_type=F32
        )

    def hop(way, part, s):
        return pltpu.make_async_remote_copy(
            snd.at[way, s, part], rcv.at[way, s, part],
            zsend.at[way, s, part], zrecv.at[way, s, part],
            device_id=(c, right if way == 0 else left), device_id_type=MESH,
        )

    for way in range(2):
        snd[way, 0] = local(way, 0).reshape(CHUNKS, rows_of, out_cols)
        for part in range(CHUNKS):
            hop(way, part, 0).start()

    def fill(s, _):
        for way in range(2):
            snd[way, s] = local(way, s).reshape(CHUNKS, rows_of, out_cols)
        return 0

    lax.fori_loop(1, nz, fill, 0)

    def ring(s, _):
        for part in range(CHUNKS):
            for way in range(2):
                hop(way, part, s - 1).wait_recv()
                snd[way, s, part] = snd[way, s, part] + rcv[way, s - 1, part]
                hop(way, part, s).start()
        return 0

    lax.fori_loop(1, nz - 1, ring, 0)
    for part in range(CHUNKS):
        for way in range(2):
            hop(way, part, nz - 2).wait_recv()
            at = way * span + part * rows_of
            o_ref[at:at + rows_of] = (snd[way, nz - 1, part] + rcv[way, nz - 2, part]).astype(BF16)

    for g in range(groups):
        each(to_owner, "wait_send", g)
        each(to_place, "wait_send", g)

    def drain(s, _):
        for way in range(2):
            for part in range(CHUNKS):
                hop(way, part, s).wait_send()
        return 0

    lax.fori_loop(0, nz - 1, drain, 0)


def solution(mesh):
    nc, nz = mesh.shape["ctx"], mesh.shape["tp"]

    def body(query, keys, values, filt, direct, w_out):
        block, chans = keys.shape
        out_cols = w_out.shape[1] // nz
        width = chans // nc
        groups = width // SUB
        rows_of = block // 2 // CHUNKS
        consts = [jnp.asarray(t) for t in tables(block)]
        operands = [query, keys, values, filt, direct.reshape(1, chans), w_out] + consts
        dma = pltpu.SemaphoreType.DMA
        return pl.pallas_call(
            functools.partial(kernel, nc, nz),
            out_shape=jax.ShapeDtypeStruct((block, out_cols), BF16),
            in_specs=[pl.BlockSpec(memory_space=pl.ANY)] * len(operands),
            out_specs=pl.BlockSpec(memory_space=pltpu.VMEM),
            scratch_shapes=[pltpu.VMEM(x.shape, x.dtype) for x in operands]
            + [
                pltpu.VMEM((groups, 2, nc, SUB, block), F32),
                pltpu.VMEM((groups, 2, nc, SUB, block), F32),
                pltpu.VMEM((2, 2, nc, SUB, LANES), F32),
                pltpu.VMEM((2, 2, nc + SUB, SUB, LANES), F32),
                pltpu.VMEM((2, 2, nc, SUB, LANES), F32),
                pltpu.VMEM((groups, nc, SUB, block), F32),
                pltpu.VMEM((chans, block), F32),
                pltpu.VMEM((block, chans), BF16),
                pltpu.VMEM((2, nz, CHUNKS, rows_of, out_cols), F32),
                pltpu.VMEM((2, nz - 1, CHUNKS, rows_of, out_cols), F32),
                dma((len(operands),)),
                dma((groups, nc)),
                dma((groups, nc)),
                dma((groups, nc)),
                dma((groups, nc)),
                dma((2, nz - 1, CHUNKS)),
                dma((2, nz - 1, CHUNKS)),
            ],
            compiler_params=pltpu.CompilerParams(
                collective_id=0, has_side_effects=True, vmem_limit_bytes=48 * 2**20
            ),
        )(*operands)

    return jax.shard_map(
        body,
        mesh=mesh,
        in_specs=(
            P("ctx", "tp"),
            P("ctx", "tp"),
            P("ctx", "tp"),
            P("ctx", "tp"),
            P("tp"),
            P("tp", None),
        ),
        out_specs=P("ctx", "tp"),
        check_vma=False,
    )
```

```python
import functools
import math

import jax
import jax.numpy as jnp
import numpy as np
from jax import lax
from jax.experimental import pallas as pl
from jax.experimental.pallas import tpu as pltpu
from jax.sharding import PartitionSpec as P

MESH = pl.DeviceIdType.MESH
F32 = jnp.float32
BF16 = jnp.bfloat16
LANES = 128
SUB = 8
PARTS = 2
SIDE = 4
NEAR = (0, 1, 2, -1)
STEPS = sorted(
    ((dx, dy, dk) for dx in NEAR for dy in NEAR for dk in (0, 1)),
    key=lambda n: (abs(n[0]) + abs(n[1]), n[2]),
)[:0:-1]


def tables(block):
    order = np.concatenate([np.arange(0, block, 2), np.arange(1, block, 2)])
    place = np.arange(block)
    angle = math.pi * (2 * order[None, :] + 1) * place[:, None] / (2 * block)
    forward = np.concatenate([np.cos(angle), -np.sin(angle)], axis=1)
    inverse = np.concatenate([np.cos(angle.T), -np.sin(angle.T)], axis=0) / block
    out = []
    for table in (forward, inverse):
        high = table.astype(jnp.bfloat16)
        low = (table - high.astype(np.float64)).astype(jnp.bfloat16)
        out += [high, low]
    return out


def split(x):
    high = x.astype(BF16)
    return high, (x - high.astype(F32)).astype(BF16)


def dot3(x, high, low):
    xh, xl = split(x)
    total = jnp.dot(xh, low, preferred_element_type=F32)
    total += jnp.dot(xl, high, preferred_element_type=F32)
    return total + jnp.dot(xh, high, preferred_element_type=F32)


def kernel(
    nc, nz,
    q_hbm, k_hbm, v_hbm, f_hbm, d_hbm, th_hbm, tl_hbm, ih_hbm, il_hbm, w_hbm,
    o_ref,
    q, k, v, f, dr, th, tl, ih, il, w,
    sbuf, rbuf, sb, gb, zb, yb, cb, gated, snd, rcv,
    lsem, asend, arecv, bsend, brecv, zsend, zrecv,
):
    c = lax.axis_index("ctx")
    z = lax.axis_index("tp")
    block, chans = k.shape
    groups = sbuf.shape[0]
    gwide = chans // groups
    out_cols = o_ref.shape[1]
    half = block // 2
    rows_of = half // PARTS

    loads = [
        pltpu.make_async_copy(src, dst, lsem.at[n])
        for n, (src, dst) in enumerate(
            [(k_hbm, k), (v_hbm, v), (f_hbm, f), (q_hbm, q), (d_hbm, dr),
             (th_hbm, th), (tl_hbm, tl), (ih_hbm, ih), (il_hbm, il), (w_hbm, w)]
        )
    ]
    for load in loads:
        load.start()

    barrier = pltpu.get_barrier_semaphore()

    def greet(d, _):
        pl.semaphore_signal(
            barrier, inc=1, device_id=(lax.rem(c + d, nc), z), device_id_type=MESH
        )
        return 0

    lax.fori_loop(1, nc, greet, 0)
    right, left = lax.rem(z + 1, nz), lax.rem(z + nz - 1, nz)
    for other in (right, left):
        pl.semaphore_signal(barrier, inc=1, device_id=(c, other), device_id_type=MESH)

    loads[0].wait()
    loads[1].wait()
    loads[2].wait()
    per = LANES // SUB
    for j in range(chans // LANES):
        cols = slice(j * LANES, (j + 1) * LANES)
        g, at = divmod(j * LANES, gwide)
        at = at // SUB
        for which in range(2):
            if which == 0:
                part = k[:, cols].astype(F32) * v[:, cols].astype(F32)
            else:
                part = f[:, cols]
            sbuf[g, which, at:at + per] = part.T.reshape(per, SUB, block)
    for g in range(groups):
        rbuf[g, :, c] = sbuf[g, :, c]
    pl.semaphore_wait(barrier, nc + 1)

    core, px, py = lax.rem(c, 2), lax.rem(c // 2, SIDE), c // (2 * SIDE)

    def partner(n):
        dx, dy, dk = STEPS[n]
        x, y = lax.rem(px + dx + SIDE, SIDE), lax.rem(py + dy + SIDE, SIDE)
        return (y * SIDE + x) * 2 + lax.rem(core + dk, 2)

    def to_owner(g, d, t):
        return pltpu.make_async_remote_copy(
            sbuf.at[g, :, t], rbuf.at[g, :, c], asend.at[g, d], arecv.at[g, d],
            device_id=(t, z), device_id_type=MESH,
        )

    def to_place(g, d, t):
        return pltpu.make_async_remote_copy(
            yb.at[g, t], cb.at[g, c], bsend.at[g, d], brecv.at[g, d],
            device_id=(t, z), device_id_type=MESH,
        )

    def each(make, act, g):
        def step(d, _):
            getattr(make(g, d, lax.rem(c + d + 1, nc)), act)()
            return 0

        lax.fori_loop(0, nc - 1, step, 0)

    def hop(way, part, s):
        return pltpu.make_async_remote_copy(
            snd.at[way, s, part], rcv.at[way, s, part],
            zsend.at[way, s, part], zrecv.at[way, s, part],
            device_id=(c, right if way == 0 else left), device_id_type=MESH,
        )

    others = [partner(n) for n in range(nc - 1)]
    for d, t in enumerate(others):
        to_owner(0, d, t).start()
    for load in loads[3:-1]:
        load.wait()
    for d, t in enumerate(others):
        to_owner(0, d, t).wait_send()
        to_owner(1, d, t).start()

    gb[:, :, 0:SUB] = jnp.zeros((2, 2, SUB, SUB, LANES), F32)

    def convolve(g):
        each(to_owner, "wait_recv", g)
        flat = (nc * SUB, block)
        spec = dot3(rbuf[g, 0].reshape(flat), th[...], tl[...])
        for part in range(2):
            for tile in range(2):
                at = part * block + tile * half
                sb[tile, part] = spec[:, at:at + half].reshape(nc, SUB, LANES)
        spec = dot3(rbuf[g, 1].reshape(flat), th[...], tl[...])
        zero = jnp.zeros((1, SUB, LANES), F32)
        for tile in range(2):
            at = tile * half
            real = spec[:, at:at + half].reshape(nc, SUB, LANES)
            imag = spec[:, block + at:block + at + half].reshape(nc, SUB, LANES)
            real_b = jnp.concatenate([zero, real[:-1]], axis=0)
            imag_b = jnp.concatenate([zero, imag[:-1]], axis=0)
            if tile == 0:
                real, imag = real - imag_b, imag + real_b
            else:
                real, imag = real + imag_b, imag - real_b
            gb[tile, 0, SUB:] = real
            gb[tile, 1, SUB:] = imag

        def combine(tile, _):
            for hi in range(nc // SUB):
                acc_r = [None] * SUB
                acc_i = [None] * SUB
                for lo in range(hi + 1):
                    srcs = [(sb[tile, 0, lo * SUB + n], sb[tile, 1, lo * SUB + n]) for n in range(SUB)]
                    base = (hi - lo) * SUB
                    for diff in range(1 - SUB, SUB):
                        if base + diff < 0:
                            continue
                        fr = gb[tile, 0, SUB + base + diff]
                        fi = gb[tile, 1, SUB + base + diff]
                        for n in range(SUB):
                            a = n + diff
                            if a < 0 or a >= SUB:
                                continue
                            sr, si = srcs[n]
                            pr = sr * fr - si * fi
                            pi = sr * fi + si * fr
                            acc_r[a] = pr if acc_r[a] is None else acc_r[a] + pr
                            acc_i[a] = pi if acc_i[a] is None else acc_i[a] + pi
                for a in range(SUB):
                    zb[0, tile, hi * SUB + a] = acc_r[a]
                    zb[1, tile, hi * SUB + a] = acc_i[a]
            return 0

        lax.fori_loop(0, 2, combine, 0)
        whole = jnp.concatenate(
            [zb[p, t].reshape(nc * SUB, LANES) for p in range(2) for t in range(2)], axis=1
        )
        yb[g] = dot3(whole, ih[...], il[...]).reshape(nc, SUB, block)
        cb[g, c] = yb[g, c]
        for d, t in enumerate(others):
            to_place(g, d, t).start()

    def receive(g):
        each(to_place, "wait_recv", g)
        for j in range(gwide // LANES):
            rows = cb[g, j * per:(j + 1) * per].reshape(LANES, block)
            cols = slice(g * gwide + j * LANES, g * gwide + (j + 1) * LANES)
            signal = k[:, cols].astype(F32) * v[:, cols].astype(F32)
            gate = q[:, cols].astype(F32) * (rows.T + dr[:, cols] * signal)
            gated[:, cols] = gate.astype(BF16)

    def local(g, way, s):
        dest = lax.rem(z + (nz - 1 - s if way == 0 else 1 + s), nz)
        cols = pl.ds(pl.multiple_of(dest * out_cols, out_cols), out_cols)
        terms = jnp.dot(
            gated[way * half:(way + 1) * half, g * gwide:(g + 1) * gwide],
            w[g * gwide:(g + 1) * gwide, cols],
            preferred_element_type=F32,
        ).reshape(PARTS, rows_of, out_cols)
        snd[way, s] = terms if g == 0 else snd[way, s] + terms

    convolve(0)
    convolve(1)
    loads[-1].wait()
    receive(0)

    def fill(s, _):
        for way in range(2):
            local(0, way, s)
        return 0

    lax.fori_loop(0, nz, fill, 0)
    receive(1)
    for way in range(2):
        local(1, way, 0)
        for part in range(PARTS):
            hop(way, part, 0).start()

    def ring(s, _):
        for way in range(2):
            local(1, way, s)
        for part in range(PARTS):
            for way in range(2):
                hop(way, part, s - 1).wait_recv()
                snd[way, s, part] = snd[way, s, part] + rcv[way, s - 1, part]
                hop(way, part, s).start()
        return 0

    lax.fori_loop(1, nz - 1, ring, 0)
    for way in range(2):
        local(1, way, nz - 1)
    for part in range(PARTS):
        for way in range(2):
            hop(way, part, nz - 2).wait_recv()
            at = way * half + part * rows_of
            o_ref[at:at + rows_of] = (snd[way, nz - 1, part] + rcv[way, nz - 2, part]).astype(BF16)

    each(to_owner, "wait_send", 1)
    for g in range(groups):
        each(to_place, "wait_send", g)

    def drain(s, _):
        for way in range(2):
            for part in range(PARTS):
                hop(way, part, s).wait_send()
        return 0

    lax.fori_loop(0, nz - 1, drain, 0)


def solution(mesh):
    nc, nz = mesh.shape["ctx"], mesh.shape["tp"]

    def body(query, keys, values, filt, direct, w_out):
        block, chans = keys.shape
        out_cols = w_out.shape[1] // nz
        groups = chans // nc // SUB
        gwide = chans // groups
        consts = [jnp.asarray(t) for t in tables(block)]
        operands = [query, keys, values, filt, direct.reshape(1, chans)] + consts + [w_out]
        rows_of = block // 2 // PARTS
        copies = [pltpu.VMEM(x.shape, x.dtype) for x in operands]
        dma = pltpu.SemaphoreType.DMA
        operands = [pltpu.with_memory_space_constraint(x, pltpu.HBM) for x in operands]
        return pl.pallas_call(
            functools.partial(kernel, nc, nz),
            out_shape=jax.ShapeDtypeStruct((block, out_cols), BF16),
            in_specs=[pl.BlockSpec(memory_space=pltpu.HBM)] * len(operands),
            out_specs=pl.BlockSpec(memory_space=pltpu.VMEM),
            scratch_shapes=copies
            + [
                pltpu.VMEM((groups, 2, nc, SUB, block), F32),
                pltpu.VMEM((groups, 2, nc, SUB, block), F32),
                pltpu.VMEM((2, 2, nc, SUB, LANES), F32),
                pltpu.VMEM((2, 2, nc + SUB, SUB, LANES), F32),
                pltpu.VMEM((2, 2, nc, SUB, LANES), F32),
                pltpu.VMEM((groups, nc, SUB, block), F32),
                pltpu.VMEM((groups, nc, SUB, block), F32),
                pltpu.VMEM((block, chans), BF16),
                pltpu.VMEM((2, nz, PARTS, rows_of, out_cols), F32),
                pltpu.VMEM((2, nz - 1, PARTS, rows_of, out_cols), F32),
                dma((len(operands),)),
                dma((groups, nc)),
                dma((groups, nc)),
                dma((groups, nc)),
                dma((groups, nc)),
                dma((2, nz - 1, PARTS)),
                dma((2, nz - 1, PARTS)),
            ],
            compiler_params=pltpu.CompilerParams(
                collective_id=0, has_side_effects=True, vmem_limit_bytes=48 * 2**20
            ),
        )(*operands)

    return jax.shard_map(
        body,
        mesh=mesh,
        in_specs=(
            P("ctx", "tp"),
            P("ctx", "tp"),
            P("ctx", "tp"),
            P("ctx", "tp"),
            P("tp"),
            P("tp", None),
        ),
        out_specs=P("ctx", "tp"),
        check_vma=False,
    )
```

```python
import functools
import math

import jax
import jax.numpy as jnp
import numpy as np
from jax import lax
from jax.experimental import pallas as pl
from jax.experimental.pallas import tpu as pltpu
from jax.sharding import PartitionSpec as P

MESH = pl.DeviceIdType.MESH
F32 = jnp.float32
BF16 = jnp.bfloat16
LANES = 128
SUB = 8
PARTS = 2
SIDE = 4
NEAR = (0, 1, 2, -1)
STEPS = sorted(
    ((dx, dy, dk) for dx in NEAR for dy in NEAR for dk in (0, 1)),
    key=lambda n: (abs(n[0]) + abs(n[1]), n[2]),
)[:0:-1]


def tables(block):
    order = np.concatenate([np.arange(0, block, 2), np.arange(1, block, 2)])
    place = np.arange(block)
    angle = math.pi * (2 * order[None, :] + 1) * place[:, None] / (2 * block)
    forward = np.concatenate([np.cos(angle), -np.sin(angle)], axis=1)
    inverse = np.concatenate([np.cos(angle.T), -np.sin(angle.T)], axis=0) / block
    out = []
    for table in (forward, inverse):
        high = table.astype(jnp.bfloat16)
        low = (table - high.astype(np.float64)).astype(jnp.bfloat16)
        out += [high, low]
    return out


def split(x):
    high = x.astype(BF16)
    return high, (x - high.astype(F32)).astype(BF16)


def dot3(x, high, low):
    xh, xl = split(x)
    total = jnp.dot(xh, low, preferred_element_type=F32)
    total += jnp.dot(xl, high, preferred_element_type=F32)
    return total + jnp.dot(xh, high, preferred_element_type=F32)


def kernel(
    nc, nz,
    q_hbm, k_hbm, v_hbm, f_hbm, d_hbm, th_hbm, tl_hbm, ih_hbm, il_hbm, w_hbm,
    o_ref,
    q, k, v, f, dr, th, tl, ih, il, w,
    sbuf, rbuf, sb, gb, zb, yb, cb, gated, snd, rcv,
    lsem, asend, arecv, bsend, brecv, zsend, zrecv,
):
    c = lax.axis_index("ctx")
    z = lax.axis_index("tp")
    block, chans = k.shape
    groups = sbuf.shape[0]
    gwide = chans // groups
    out_cols = o_ref.shape[1]
    half = block // 2
    rows_of = half // PARTS

    loads = [
        pltpu.make_async_copy(src, dst, lsem.at[n])
        for n, (src, dst) in enumerate(
            [(k_hbm, k), (v_hbm, v), (f_hbm, f), (q_hbm, q), (d_hbm, dr),
             (th_hbm, th), (tl_hbm, tl), (ih_hbm, ih), (il_hbm, il), (w_hbm, w)]
        )
    ]
    for load in loads[:3]:
        load.start()

    barrier = pltpu.get_barrier_semaphore()

    def greet(d, _):
        pl.semaphore_signal(
            barrier, inc=1, device_id=(lax.rem(c + d, nc), z), device_id_type=MESH
        )
        return 0

    lax.fori_loop(1, nc, greet, 0)
    right, left = lax.rem(z + 1, nz), lax.rem(z + nz - 1, nz)
    for other in (right, left):
        pl.semaphore_signal(barrier, inc=1, device_id=(c, other), device_id_type=MESH)

    loads[0].wait()
    loads[1].wait()
    loads[2].wait()
    per = LANES // SUB
    for j in range(chans // LANES):
        cols = slice(j * LANES, (j + 1) * LANES)
        g, at = divmod(j * LANES, gwide)
        at = at // SUB
        for which in range(2):
            if which == 0:
                part = k[:, cols].astype(F32) * v[:, cols].astype(F32)
            else:
                part = f[:, cols]
            sbuf[g, which, at:at + per] = part.T.reshape(per, SUB, block)
    for g in range(groups):
        rbuf[g, :, c] = sbuf[g, :, c]
    pl.semaphore_wait(barrier, nc + 1)

    core, px, py = lax.rem(c, 2), lax.rem(c // 2, SIDE), c // (2 * SIDE)

    def partner(n):
        dx, dy, dk = STEPS[n]
        x, y = lax.rem(px + dx + SIDE, SIDE), lax.rem(py + dy + SIDE, SIDE)
        return (y * SIDE + x) * 2 + lax.rem(core + dk, 2)

    def to_owner(g, t):
        return pltpu.make_async_remote_copy(
            sbuf.at[g, :, t], rbuf.at[g, :, c], asend.at[g], arecv.at[g],
            device_id=(t, z), device_id_type=MESH,
        )

    def to_place(g, t):
        return pltpu.make_async_remote_copy(
            yb.at[g, t], cb.at[g, c], bsend.at[g], brecv.at[g],
            device_id=(t, z), device_id_type=MESH,
        )

    def all_owner(g):
        blocks = pl.ds(0, nc - 1)
        return pltpu.make_async_remote_copy(
            sbuf.at[g, :, blocks], rbuf.at[g, :, blocks], asend.at[g], arecv.at[g],
            device_id=(others[0], z), device_id_type=MESH,
        )

    def all_place(g):
        blocks = pl.ds(0, nc - 1)
        return pltpu.make_async_remote_copy(
            yb.at[g, blocks], cb.at[g, blocks], bsend.at[g], brecv.at[g],
            device_id=(others[0], z), device_id_type=MESH,
        )

    def all_hops():
        steps = pl.ds(0, nz - 1)
        return pltpu.make_async_remote_copy(
            snd.at[:, steps], rcv, zsend.at[0], zrecv.at[0, 0, 0],
            device_id=(c, right), device_id_type=MESH,
        )

    def hop(way, part, s):
        return pltpu.make_async_remote_copy(
            snd.at[way, s, part], rcv.at[way, s, part],
            zsend.at[0], zrecv.at[way, s, part],
            device_id=(c, right if way == 0 else left), device_id_type=MESH,
        )

    others = [partner(n) for n in range(nc - 1)]
    for t in others:
        to_owner(0, t).start()
    for load in loads[3:]:
        load.start()
    for load in loads[3:-1]:
        load.wait()
    all_owner(0).wait_send()
    for t in others:
        to_owner(1, t).start()

    gb[:, :, 0:SUB] = jnp.zeros((2, 2, SUB, SUB, LANES), F32)

    def convolve(g):
        all_owner(g).wait_recv()
        flat = (nc * SUB, block)
        spec = dot3(rbuf[g, 0].reshape(flat), th[...], tl[...])
        for part in range(2):
            for tile in range(2):
                at = part * block + tile * half
                sb[tile, part] = spec[:, at:at + half].reshape(nc, SUB, LANES)
        spec = dot3(rbuf[g, 1].reshape(flat), th[...], tl[...])
        zero = jnp.zeros((1, SUB, LANES), F32)
        for tile in range(2):
            at = tile * half
            real = spec[:, at:at + half].reshape(nc, SUB, LANES)
            imag = spec[:, block + at:block + at + half].reshape(nc, SUB, LANES)
            real_b = jnp.concatenate([zero, real[:-1]], axis=0)
            imag_b = jnp.concatenate([zero, imag[:-1]], axis=0)
            if tile == 0:
                real, imag = real - imag_b, imag + real_b
            else:
                real, imag = real + imag_b, imag - real_b
            gb[tile, 0, SUB:] = real
            gb[tile, 1, SUB:] = imag

        def combine(tile, _):
            for hi in range(nc // SUB):
                acc_r = [None] * SUB
                acc_i = [None] * SUB
                for lo in range(hi + 1):
                    srcs = [(sb[tile, 0, lo * SUB + n], sb[tile, 1, lo * SUB + n]) for n in range(SUB)]
                    base = (hi - lo) * SUB
                    for diff in range(1 - SUB, SUB):
                        if base + diff < 0:
                            continue
                        fr = gb[tile, 0, SUB + base + diff]
                        fi = gb[tile, 1, SUB + base + diff]
                        for n in range(SUB):
                            a = n + diff
                            if a < 0 or a >= SUB:
                                continue
                            sr, si = srcs[n]
                            pr = sr * fr - si * fi
                            pi = sr * fi + si * fr
                            acc_r[a] = pr if acc_r[a] is None else acc_r[a] + pr
                            acc_i[a] = pi if acc_i[a] is None else acc_i[a] + pi
                for a in range(SUB):
                    zb[0, tile, hi * SUB + a] = acc_r[a]
                    zb[1, tile, hi * SUB + a] = acc_i[a]
            return 0

        lax.fori_loop(0, 2, combine, 0)
        whole = jnp.concatenate(
            [zb[p, t].reshape(nc * SUB, LANES) for p in range(2) for t in range(2)], axis=1
        )
        yb[g] = dot3(whole, ih[...], il[...]).reshape(nc, SUB, block)
        cb[g, c] = yb[g, c]
        for t in others:
            to_place(g, t).start()

    def receive(g):
        all_place(g).wait_recv()
        for j in range(gwide // LANES):
            rows = cb[g, j * per:(j + 1) * per].reshape(LANES, block)
            cols = slice(g * gwide + j * LANES, g * gwide + (j + 1) * LANES)
            signal = k[:, cols].astype(F32) * v[:, cols].astype(F32)
            gate = q[:, cols].astype(F32) * (rows.T + dr[:, cols] * signal)
            gated[:, cols] = gate.astype(BF16)

    def local(g, way, s):
        dest = lax.rem(z + (nz - 1 - s if way == 0 else 1 + s), nz)
        cols = pl.ds(pl.multiple_of(dest * out_cols, out_cols), out_cols)
        terms = jnp.dot(
            gated[way * half:(way + 1) * half, g * gwide:(g + 1) * gwide],
            w[g * gwide:(g + 1) * gwide, cols],
            preferred_element_type=F32,
        ).reshape(PARTS, rows_of, out_cols)
        snd[way, s] = terms if g == 0 else snd[way, s] + terms

    convolve(0)
    convolve(1)
    loads[-1].wait()
    receive(0)

    def fill(s, _):
        for way in range(2):
            local(0, way, s)
        return 0

    lax.fori_loop(0, nz, fill, 0)
    receive(1)
    for way in range(2):
        local(1, way, 0)
        for part in range(PARTS):
            hop(way, part, 0).start()

    def ring(s, _):
        for way in range(2):
            local(1, way, s)
        for part in range(PARTS):
            for way in range(2):
                hop(way, part, s - 1).wait_recv()
                snd[way, s, part] = snd[way, s, part] + rcv[way, s - 1, part]
                hop(way, part, s).start()
        return 0

    lax.fori_loop(1, nz - 1, ring, 0)
    for way in range(2):
        local(1, way, nz - 1)
    for part in range(PARTS):
        for way in range(2):
            hop(way, part, nz - 2).wait_recv()
            at = way * half + part * rows_of
            o_ref[at:at + rows_of] = (snd[way, nz - 1, part] + rcv[way, nz - 2, part]).astype(BF16)

    all_owner(1).wait_send()
    for g in range(groups):
        all_place(g).wait_send()
    all_hops().wait_send()


def solution(mesh):
    nc, nz = mesh.shape["ctx"], mesh.shape["tp"]

    def body(query, keys, values, filt, direct, w_out):
        block, chans = keys.shape
        out_cols = w_out.shape[1] // nz
        groups = chans // nc // SUB
        gwide = chans // groups
        consts = [jnp.asarray(t) for t in tables(block)]
        operands = [query, keys, values, filt, direct.reshape(1, chans)] + consts + [w_out]
        rows_of = block // 2 // PARTS
        copies = [pltpu.VMEM(x.shape, x.dtype) for x in operands]
        dma = pltpu.SemaphoreType.DMA
        operands = [pltpu.with_memory_space_constraint(x, pltpu.HBM) for x in operands]
        return pl.pallas_call(
            functools.partial(kernel, nc, nz),
            out_shape=jax.ShapeDtypeStruct((block, out_cols), BF16),
            in_specs=[pl.BlockSpec(memory_space=pltpu.HBM)] * len(operands),
            out_specs=pl.BlockSpec(memory_space=pltpu.VMEM),
            scratch_shapes=copies
            + [
                pltpu.VMEM((groups, 2, nc, SUB, block), F32),
                pltpu.VMEM((groups, 2, nc, SUB, block), F32),
                pltpu.VMEM((2, 2, nc, SUB, LANES), F32),
                pltpu.VMEM((2, 2, nc + SUB, SUB, LANES), F32),
                pltpu.VMEM((2, 2, nc, SUB, LANES), F32),
                pltpu.VMEM((groups, nc, SUB, block), F32),
                pltpu.VMEM((groups, nc, SUB, block), F32),
                pltpu.VMEM((block, chans), BF16),
                pltpu.VMEM((2, nz, PARTS, rows_of, out_cols), F32),
                pltpu.VMEM((2, nz - 1, PARTS, rows_of, out_cols), F32),
                dma((len(operands),)),
                dma((groups,)),
                dma((groups,)),
                dma((groups,)),
                dma((groups,)),
                dma((1,)),
                dma((2, nz - 1, PARTS)),
            ],
            compiler_params=pltpu.CompilerParams(
                collective_id=0, has_side_effects=True, vmem_limit_bytes=48 * 2**20
            ),
        )(*operands)

    return jax.shard_map(
        body,
        mesh=mesh,
        in_specs=(
            P("ctx", "tp"),
            P("ctx", "tp"),
            P("ctx", "tp"),
            P("ctx", "tp"),
            P("tp"),
            P("tp", None),
        ),
        out_specs=P("ctx", "tp"),
        check_vma=False,
    )
```

```python
import functools
import math

import jax
import jax.numpy as jnp
import numpy as np
from jax import lax
from jax.experimental import pallas as pl
from jax.experimental.pallas import tpu as pltpu
from jax.sharding import PartitionSpec as P

MESH = pl.DeviceIdType.MESH
F32 = jnp.float32
BF16 = jnp.bfloat16
LANES = 128
SUB = 8
PARTS = 2
SIDE = 4
NEAR = (0, 1, 2, -1)
STEPS = sorted(
    ((dx, dy, dk) for dx in NEAR for dy in NEAR for dk in (0, 1)),
    key=lambda n: (abs(n[0]) + abs(n[1]), n[2]),
)[:0:-1]


def tables(block):
    order = np.concatenate([np.arange(0, block, 2), np.arange(1, block, 2)])
    place = np.arange(block)
    angle = math.pi * (2 * order[None, :] + 1) * place[:, None] / (2 * block)
    forward = np.concatenate([np.cos(angle), -np.sin(angle)], axis=1)
    inverse = np.concatenate([np.cos(angle.T), -np.sin(angle.T)], axis=0) / block
    out = []
    for table in (forward, inverse):
        high = table.astype(jnp.bfloat16)
        low = (table - high.astype(np.float64)).astype(jnp.bfloat16)
        out += [high, low]
    return out


def split(x):
    high = x.astype(BF16)
    return high, (x - high.astype(F32)).astype(BF16)


def dot3(x, high, low):
    xh, xl = split(x)
    total = jnp.dot(xh, low, preferred_element_type=F32)
    total += jnp.dot(xl, high, preferred_element_type=F32)
    return total + jnp.dot(xh, high, preferred_element_type=F32)


def kernel(
    nc, nz,
    q_hbm, k_hbm, v_hbm, f_hbm, d_hbm, th_hbm, tl_hbm, ih_hbm, il_hbm, w_hbm,
    o_ref,
    q, k, v, f, dr, th, tl, ih, il, w,
    sbuf, rbuf, sb, gb, zb, yb, cb, gated, snd, rcv, wown, wfar, wnext, gown, gfar,
    lsem, asend, arecv, bsend, brecv, zsend, zrecv, wsend, wrecv, gsend, grecv,
):
    c = lax.axis_index("ctx")
    z = lax.axis_index("tp")
    block, chans = k.shape
    groups = sbuf.shape[0]
    gwide = chans // groups
    out_cols = o_ref.shape[1]
    half = block // 2
    rows_of = half // PARTS

    loads = [
        pltpu.make_async_copy(src, dst, lsem.at[n])
        for n, (src, dst) in enumerate(
            [(k_hbm, k), (v_hbm, v), (f_hbm, f), (q_hbm, q), (d_hbm, dr),
             (th_hbm, th), (tl_hbm, tl), (ih_hbm, ih), (il_hbm, il), (w_hbm, w)]
        )
    ]
    for load in loads[:3]:
        load.start()

    barrier = pltpu.get_barrier_semaphore()

    def greet(d, _):
        pl.semaphore_signal(
            barrier, inc=1, device_id=(lax.rem(c + d, nc), z), device_id_type=MESH
        )
        return 0

    lax.fori_loop(1, nc, greet, 0)
    right, left = lax.rem(z + 1, nz), lax.rem(z + nz - 1, nz)
    for other in (right, left):
        pl.semaphore_signal(barrier, inc=1, device_id=(c, other), device_id_type=MESH)

    loads[0].wait()
    loads[1].wait()
    loads[2].wait()
    per = LANES // SUB
    for j in range(chans // LANES):
        cols = slice(j * LANES, (j + 1) * LANES)
        g, at = divmod(j * LANES, gwide)
        at = at // SUB
        for which in range(2):
            if which == 0:
                part = k[:, cols].astype(F32) * v[:, cols].astype(F32)
            else:
                part = f[:, cols]
            sbuf[g, which, at:at + per] = part.T.reshape(per, SUB, block)
    for g in range(groups):
        rbuf[g, :, c] = sbuf[g, :, c]
    pl.semaphore_wait(barrier, nc + 1)

    core, px, py = lax.rem(c, 2), lax.rem(c // 2, SIDE), c // (2 * SIDE)

    def partner(n):
        dx, dy, dk = STEPS[n]
        x, y = lax.rem(px + dx + SIDE, SIDE), lax.rem(py + dy + SIDE, SIDE)
        return (y * SIDE + x) * 2 + lax.rem(core + dk, 2)

    def to_owner(g, t):
        return pltpu.make_async_remote_copy(
            sbuf.at[g, :, t], rbuf.at[g, :, c], asend.at[g], arecv.at[g],
            device_id=(t, z), device_id_type=MESH,
        )

    def to_place(g, t):
        return pltpu.make_async_remote_copy(
            yb.at[g, t], cb.at[g, c], bsend.at[g], brecv.at[g],
            device_id=(t, z), device_id_type=MESH,
        )

    def all_owner(g):
        blocks = pl.ds(0, nc - 1)
        return pltpu.make_async_remote_copy(
            sbuf.at[g, :, blocks], rbuf.at[g, :, blocks], asend.at[g], arecv.at[g],
            device_id=(others[0], z), device_id_type=MESH,
        )

    def all_place(g):
        blocks = pl.ds(0, nc - 1)
        return pltpu.make_async_remote_copy(
            yb.at[g, blocks], cb.at[g, blocks], bsend.at[g], brecv.at[g],
            device_id=(others[0], z), device_id_type=MESH,
        )

    def all_hops():
        steps = pl.ds(1, nz - 2)
        return pltpu.make_async_remote_copy(
            snd.at[:, steps], rcv.at[:, steps], zsend.at[0], zrecv.at[0, 0, 0],
            device_id=(c, right), device_id_type=MESH,
        )

    def hop(way, part, s):
        return pltpu.make_async_remote_copy(
            snd.at[way, s, part], rcv.at[way, s, part],
            zsend.at[0], zrecv.at[way, s - 1, part],
            device_id=(c, right if way == 0 else left), device_id_type=MESH,
        )

    sibling = c + 1 - 2 * core
    wrows = pl.ds(pl.multiple_of(core * gwide, gwide), gwide)

    def block_of(step):
        at = lax.rem(z + nz + step, nz) * out_cols
        return pl.ds(pl.multiple_of(at, out_cols), out_cols)

    def to_next(way):
        return pltpu.make_async_remote_copy(
            wown.at[way], wfar.at[way, wrows], wsend.at[way], wrecv.at[way],
            device_id=(c, right if way == 0 else left), device_id_type=MESH,
        )

    def to_sibling():
        rows = wfar.at[:, wrows]
        return pltpu.make_async_remote_copy(
            rows, rows, wsend.at[2], wrecv.at[2], device_id=(sibling, z), device_id_type=MESH
        )

    def gated_hop(way, g, part):
        return pltpu.make_async_remote_copy(
            gown.at[way, g, part], gfar.at[way, g, part],
            gsend.at[0], grecv.at[way, g, part],
            device_id=(c, right if way == 0 else left), device_id_type=MESH,
        )

    def all_gated():
        return pltpu.make_async_remote_copy(
            gown, gfar, gsend.at[0], grecv.at[0, 0, 0],
            device_id=(c, right), device_id_type=MESH,
        )

    others = [partner(n) for n in range(nc - 1)]
    for t in others:
        to_owner(0, t).start()
    for load in loads[3:]:
        load.start()
    for load in loads[3:-1]:
        load.wait()
    all_owner(0).wait_send()
    for t in others:
        to_owner(1, t).start()
    loads[-1].wait()
    for way in range(2):
        wown[way] = w[wrows, block_of(1 if way else -1)].astype(F32)
        to_next(way).start()

    gb[:, :, 0:SUB] = jnp.zeros((2, 2, SUB, SUB, LANES), F32)

    def convolve(g):
        all_owner(g).wait_recv()
        flat = (nc * SUB, block)
        spec = dot3(rbuf[g, 0].reshape(flat), th[...], tl[...])
        for part in range(2):
            for tile in range(2):
                at = part * block + tile * half
                sb[tile, part] = spec[:, at:at + half].reshape(nc, SUB, LANES)
        spec = dot3(rbuf[g, 1].reshape(flat), th[...], tl[...])
        zero = jnp.zeros((1, SUB, LANES), F32)
        for tile in range(2):
            at = tile * half
            real = spec[:, at:at + half].reshape(nc, SUB, LANES)
            imag = spec[:, block + at:block + at + half].reshape(nc, SUB, LANES)
            real_b = jnp.concatenate([zero, real[:-1]], axis=0)
            imag_b = jnp.concatenate([zero, imag[:-1]], axis=0)
            if tile == 0:
                real, imag = real - imag_b, imag + real_b
            else:
                real, imag = real + imag_b, imag - real_b
            gb[tile, 0, SUB:] = real
            gb[tile, 1, SUB:] = imag

        def combine(tile, _):
            for hi in range(nc // SUB):
                acc_r = [None] * SUB
                acc_i = [None] * SUB
                for lo in range(hi + 1):
                    srcs = [(sb[tile, 0, lo * SUB + n], sb[tile, 1, lo * SUB + n]) for n in range(SUB)]
                    base = (hi - lo) * SUB
                    for diff in range(1 - SUB, SUB):
                        if base + diff < 0:
                            continue
                        fr = gb[tile, 0, SUB + base + diff]
                        fi = gb[tile, 1, SUB + base + diff]
                        for n in range(SUB):
                            a = n + diff
                            if a < 0 or a >= SUB:
                                continue
                            sr, si = srcs[n]
                            pr = sr * fr - si * fi
                            pi = sr * fi + si * fr
                            acc_r[a] = pr if acc_r[a] is None else acc_r[a] + pr
                            acc_i[a] = pi if acc_i[a] is None else acc_i[a] + pi
                for a in range(SUB):
                    zb[0, tile, hi * SUB + a] = acc_r[a]
                    zb[1, tile, hi * SUB + a] = acc_i[a]
            return 0

        lax.fori_loop(0, 2, combine, 0)
        whole = jnp.concatenate(
            [zb[p, t].reshape(nc * SUB, LANES) for p in range(2) for t in range(2)], axis=1
        )
        yb[g] = dot3(whole, ih[...], il[...]).reshape(nc, SUB, block)
        cb[g, c] = yb[g, c]
        for t in others:
            to_place(g, t).start()

    def receive(g):
        all_place(g).wait_recv()
        for j in range(gwide // LANES):
            rows = cb[g, j * per:(j + 1) * per].reshape(LANES, block)
            cols = slice(g * gwide + j * LANES, g * gwide + (j + 1) * LANES)
            signal = k[:, cols].astype(F32) * v[:, cols].astype(F32)
            gate = q[:, cols].astype(F32) * (rows.T + dr[:, cols] * signal)
            gate = gate.astype(BF16)
            gated[:, cols] = gate
            gate = gate.astype(F32).reshape(2, PARTS, rows_of, LANES)
            gown[:, g, :, :, j * LANES:(j + 1) * LANES] = gate
        for part in range(PARTS):
            for way in range(2):
                gated_hop(way, g, part).start()

    def local(g, way, s):
        dest = lax.rem(z + (nz - 1 - s if way == 0 else 1 + s), nz)
        cols = pl.ds(pl.multiple_of(dest * out_cols, out_cols), out_cols)
        terms = jnp.dot(
            gated[way * half:(way + 1) * half, g * gwide:(g + 1) * gwide],
            w[g * gwide:(g + 1) * gwide, cols],
            preferred_element_type=F32,
        ).reshape(PARTS, rows_of, out_cols)
        snd[way, s] = terms if g == 0 else snd[way, s] + terms

    convolve(0)
    convolve(1)
    for way in range(2):
        to_next(way).wait_recv()
    to_sibling().start()
    receive(0)

    def fill(s, _):
        for way in range(2):
            local(0, way, s)
        return 0

    lax.fori_loop(1, nz, fill, 0)
    to_sibling().wait_recv()
    wnext[...] = wfar[...].astype(BF16)
    for way in range(2):
        for part in range(PARTS):
            gated_hop(way, 0, part).wait_recv()
            snd[way, 1, part] = snd[way, 1, part] + jnp.dot(
                gfar[way, 0, part].astype(BF16), wnext[way, :gwide], preferred_element_type=F32
            )
    receive(1)
    for way in range(2):
        local(1, way, 1)
    for part in range(PARTS):
        for way in range(2):
            gated_hop(way, 1, part).wait_recv()
            snd[way, 1, part] = snd[way, 1, part] + jnp.dot(
                gfar[way, 1, part].astype(BF16), wnext[way, gwide:], preferred_element_type=F32
            )
            hop(way, part, 1).start()

    def ring(s, _):
        for way in range(2):
            local(1, way, s)
        for part in range(PARTS):
            for way in range(2):
                hop(way, part, s - 1).wait_recv()
                snd[way, s, part] = snd[way, s, part] + rcv[way, s - 1, part]
                hop(way, part, s).start()
        return 0

    lax.fori_loop(2, nz - 1, ring, 0)
    for way in range(2):
        local(1, way, nz - 1)
    for part in range(PARTS):
        for way in range(2):
            hop(way, part, nz - 2).wait_recv()
            at = way * half + part * rows_of
            o_ref[at:at + rows_of] = (snd[way, nz - 1, part] + rcv[way, nz - 2, part]).astype(BF16)

    all_owner(1).wait_send()
    for g in range(groups):
        all_place(g).wait_send()
    all_hops().wait_send()
    all_gated().wait_send()
    for way in range(2):
        to_next(way).wait_send()
    to_sibling().wait_send()


def solution(mesh):
    nc, nz = mesh.shape["ctx"], mesh.shape["tp"]

    def body(query, keys, values, filt, direct, w_out):
        block, chans = keys.shape
        out_cols = w_out.shape[1] // nz
        groups = chans // nc // SUB
        gwide = chans // groups
        consts = [jnp.asarray(t) for t in tables(block)]
        operands = [query, keys, values, filt, direct.reshape(1, chans)] + consts + [w_out]
        rows_of = block // 2 // PARTS
        copies = [pltpu.VMEM(x.shape, x.dtype) for x in operands]
        dma = pltpu.SemaphoreType.DMA
        operands = [pltpu.with_memory_space_constraint(x, pltpu.HBM) for x in operands]
        return pl.pallas_call(
            functools.partial(kernel, nc, nz),
            out_shape=jax.ShapeDtypeStruct((block, out_cols), BF16),
            in_specs=[pl.BlockSpec(memory_space=pltpu.HBM)] * len(operands),
            out_specs=pl.BlockSpec(memory_space=pltpu.VMEM),
            scratch_shapes=copies
            + [
                pltpu.VMEM((groups, 2, nc, SUB, block), F32),
                pltpu.VMEM((groups, 2, nc, SUB, block), F32),
                pltpu.VMEM((2, 2, nc, SUB, LANES), F32),
                pltpu.VMEM((2, 2, nc + SUB, SUB, LANES), F32),
                pltpu.VMEM((2, 2, nc, SUB, LANES), F32),
                pltpu.VMEM((groups, nc, SUB, block), F32),
                pltpu.VMEM((groups, nc, SUB, block), F32),
                pltpu.VMEM((block, chans), BF16),
                pltpu.VMEM((2, nz, PARTS, rows_of, out_cols), F32),
                pltpu.VMEM((2, nz - 1, PARTS, rows_of, out_cols), F32),
                pltpu.VMEM((2, gwide, out_cols), F32),
                pltpu.VMEM((2, chans, out_cols), F32),
                pltpu.VMEM((2, chans, out_cols), BF16),
                pltpu.VMEM((2, groups, PARTS, rows_of, gwide), F32),
                pltpu.VMEM((2, groups, PARTS, rows_of, gwide), F32),
                dma((len(operands),)),
                dma((groups,)),
                dma((groups,)),
                dma((groups,)),
                dma((groups,)),
                dma((1,)),
                dma((2, nz - 2, PARTS)),
                dma((3,)),
                dma((3,)),
                dma((1,)),
                dma((2, groups, PARTS)),
            ],
            compiler_params=pltpu.CompilerParams(
                collective_id=0, has_side_effects=True, vmem_limit_bytes=48 * 2**20
            ),
        )(*operands)

    return jax.shard_map(
        body,
        mesh=mesh,
        in_specs=(
            P("ctx", "tp"),
            P("ctx", "tp"),
            P("ctx", "tp"),
            P("ctx", "tp"),
            P("tp"),
            P("tp", None),
        ),
        out_specs=P("ctx", "tp"),
        check_vma=False,
    )
```

```python
import functools
import math

import jax
import jax.numpy as jnp
import numpy as np
from jax import lax
from jax.experimental import pallas as pl
from jax.experimental.pallas import tpu as pltpu
from jax.sharding import PartitionSpec as P

MESH = pl.DeviceIdType.MESH
F32 = jnp.float32
BF16 = jnp.bfloat16
LANES = 128
SUB = 8
PARTS = 4
SIDE = 4
NEAR = (0, 1, 2, -1)
STEPS = sorted(
    ((dx, dy, dk) for dx in NEAR for dy in NEAR for dk in (0, 1)),
    key=lambda n: (abs(n[0]) + abs(n[1]), n[2]),
)[:0:-1]


def tables(block):
    order = np.concatenate([np.arange(0, block, 2), np.arange(1, block, 2)])
    place = np.arange(block)
    angle = math.pi * (2 * order[None, :] + 1) * place[:, None] / (2 * block)
    forward = np.concatenate([np.cos(angle), -np.sin(angle)], axis=1)
    inverse = np.concatenate([np.cos(angle.T), -np.sin(angle.T)], axis=0) / block
    out = []
    for table in (forward, inverse):
        high = table.astype(jnp.bfloat16)
        low = (table - high.astype(np.float64)).astype(jnp.bfloat16)
        out += [high, low]
    return out


def split(x):
    high = x.astype(BF16)
    return high, (x - high.astype(F32)).astype(BF16)


def dot3(x, high, low):
    xh, xl = split(x)
    total = jnp.dot(xh, low, preferred_element_type=F32)
    total += jnp.dot(xl, high, preferred_element_type=F32)
    return total + jnp.dot(xh, high, preferred_element_type=F32)


def kernel(
    nc, nz,
    q_hbm, k_hbm, v_hbm, f_hbm, d_hbm, th_hbm, tl_hbm, ih_hbm, il_hbm, w_hbm,
    o_ref,
    q, k, v, f, dr, th, tl, ih, il, w,
    sbuf, rbuf, sb, gb, zb, yb, cb, gated, snd, rcv, wpart, wown, wfar, wnext, gown, gfar,
    lsem, asend, arecv, bsend, brecv, zsend, zrecv, wsend, wrecv, gsend, grecv,
):
    c = lax.axis_index("ctx")
    z = lax.axis_index("tp")
    block, chans = k.shape
    groups = sbuf.shape[0]
    gwide = chans // groups
    out_cols = o_ref.shape[1]
    half = block // 2
    rows_of = half // PARTS

    core, px, py = lax.rem(c, 2), lax.rem(c // 2, SIDE), c // (2 * SIDE)

    sibling = c + 1 - 2 * core
    wrows = pl.ds(pl.multiple_of(core * gwide, gwide), gwide)

    def block_of(step):
        at = lax.rem(z + nz + step, nz) * out_cols
        return pl.ds(pl.multiple_of(at, out_cols), out_cols)

    loads = [
        pltpu.make_async_copy(src, dst, lsem.at[n])
        for n, (src, dst) in enumerate(
            [(k_hbm, k), (v_hbm, v), (f_hbm, f), (q_hbm, q), (d_hbm, dr),
             (th_hbm, th), (tl_hbm, tl), (ih_hbm, ih), (il_hbm, il), (w_hbm, w)]
        )
    ]
    first = [
        pltpu.make_async_copy(
            w_hbm.at[wrows, block_of(1 if way else -1)], wpart.at[way], lsem.at[len(loads) + way]
        )
        for way in range(2)
    ]
    for load in loads[:3] + first:
        load.start()

    barrier = pltpu.get_barrier_semaphore()

    def greet(d, _):
        pl.semaphore_signal(
            barrier, inc=1, device_id=(lax.rem(c + d, nc), z), device_id_type=MESH
        )
        return 0

    lax.fori_loop(1, nc, greet, 0)
    right, left = lax.rem(z + 1, nz), lax.rem(z + nz - 1, nz)
    for other in (right, left):
        pl.semaphore_signal(barrier, inc=1, device_id=(c, other), device_id_type=MESH)

    loads[0].wait()
    loads[1].wait()
    loads[2].wait()
    per = LANES // SUB
    for j in range(chans // LANES):
        cols = slice(j * LANES, (j + 1) * LANES)
        g, at = divmod(j * LANES, gwide)
        at = at // SUB
        for which in range(2):
            if which == 0:
                part = k[:, cols].astype(F32) * v[:, cols].astype(F32)
            else:
                part = f[:, cols]
            sbuf[g, which, at:at + per] = part.T.reshape(per, SUB, block)
    for g in range(groups):
        rbuf[g, :, c] = sbuf[g, :, c]
    for way in range(2):
        first[way].wait()
        wown[way] = wpart[way].astype(F32)
    pl.semaphore_wait(barrier, nc + 1)

    def partner(n):
        dx, dy, dk = STEPS[n]
        x, y = lax.rem(px + dx + SIDE, SIDE), lax.rem(py + dy + SIDE, SIDE)
        return (y * SIDE + x) * 2 + lax.rem(core + dk, 2)

    def to_owner(g, t):
        return pltpu.make_async_remote_copy(
            sbuf.at[g, :, t], rbuf.at[g, :, c], asend.at[g], arecv.at[g],
            device_id=(t, z), device_id_type=MESH,
        )

    def to_place(g, t):
        return pltpu.make_async_remote_copy(
            yb.at[g, t], cb.at[g, c], bsend.at[g], brecv.at[g],
            device_id=(t, z), device_id_type=MESH,
        )

    def all_owner(g):
        blocks = pl.ds(0, nc - 1)
        return pltpu.make_async_remote_copy(
            sbuf.at[g, :, blocks], rbuf.at[g, :, blocks], asend.at[g], arecv.at[g],
            device_id=(others[0], z), device_id_type=MESH,
        )

    def all_place(g):
        blocks = pl.ds(0, nc - 1)
        return pltpu.make_async_remote_copy(
            yb.at[g, blocks], cb.at[g, blocks], bsend.at[g], brecv.at[g],
            device_id=(others[0], z), device_id_type=MESH,
        )

    def all_hops():
        steps = pl.ds(1, nz - 2)
        return pltpu.make_async_remote_copy(
            snd.at[:, steps], rcv.at[:, steps], zsend.at[0], zrecv.at[0, 0, 0],
            device_id=(c, right), device_id_type=MESH,
        )

    def hop(way, part, s):
        return pltpu.make_async_remote_copy(
            snd.at[way, s, part], rcv.at[way, s, part],
            zsend.at[0], zrecv.at[way, s - 1, part],
            device_id=(c, right if way == 0 else left), device_id_type=MESH,
        )

    def to_next(way):
        return pltpu.make_async_remote_copy(
            wown.at[way], wfar.at[way, wrows], wsend.at[way], wrecv.at[way],
            device_id=(c, right if way == 0 else left), device_id_type=MESH,
        )

    def to_sibling():
        rows = wfar.at[:, wrows]
        return pltpu.make_async_remote_copy(
            rows, rows, wsend.at[2], wrecv.at[2], device_id=(sibling, z), device_id_type=MESH
        )

    def gated_hop(way, g, part):
        return pltpu.make_async_remote_copy(
            gown.at[way, g, part], gfar.at[way, g, part],
            gsend.at[0], grecv.at[way, g, part],
            device_id=(c, right if way == 0 else left), device_id_type=MESH,
        )

    def all_gated():
        return pltpu.make_async_remote_copy(
            gown, gfar, gsend.at[0], grecv.at[0, 0, 0],
            device_id=(c, right), device_id_type=MESH,
        )

    others = [partner(n) for n in range(nc - 1)]
    for t in others:
        to_owner(0, t).start()
    for way in range(2):
        to_next(way).start()
    for load in loads[3:]:
        load.start()
    for load in loads[3:-1]:
        load.wait()
    all_owner(0).wait_send()
    for t in others:
        to_owner(1, t).start()

    gb[:, :, 0:SUB] = jnp.zeros((2, 2, SUB, SUB, LANES), F32)

    def convolve(g):
        all_owner(g).wait_recv()
        flat = (nc * SUB, block)
        spec = dot3(rbuf[g, 0].reshape(flat), th[...], tl[...])
        for part in range(2):
            for tile in range(2):
                at = part * block + tile * half
                sb[tile, part] = spec[:, at:at + half].reshape(nc, SUB, LANES)
        spec = dot3(rbuf[g, 1].reshape(flat), th[...], tl[...])
        zero = jnp.zeros((1, SUB, LANES), F32)
        for tile in range(2):
            at = tile * half
            real = spec[:, at:at + half].reshape(nc, SUB, LANES)
            imag = spec[:, block + at:block + at + half].reshape(nc, SUB, LANES)
            real_b = jnp.concatenate([zero, real[:-1]], axis=0)
            imag_b = jnp.concatenate([zero, imag[:-1]], axis=0)
            if tile == 0:
                real, imag = real - imag_b, imag + real_b
            else:
                real, imag = real + imag_b, imag - real_b
            gb[tile, 0, SUB:] = real
            gb[tile, 1, SUB:] = imag

        def combine(tile, _):
            for hi in range(nc // SUB):
                acc_r = [None] * SUB
                acc_i = [None] * SUB
                for lo in range(hi + 1):
                    srcs = [(sb[tile, 0, lo * SUB + n], sb[tile, 1, lo * SUB + n]) for n in range(SUB)]
                    base = (hi - lo) * SUB
                    for diff in range(1 - SUB, SUB):
                        if base + diff < 0:
                            continue
                        fr = gb[tile, 0, SUB + base + diff]
                        fi = gb[tile, 1, SUB + base + diff]
                        for n in range(SUB):
                            a = n + diff
                            if a < 0 or a >= SUB:
                                continue
                            sr, si = srcs[n]
                            pr = sr * fr - si * fi
                            pi = sr * fi + si * fr
                            acc_r[a] = pr if acc_r[a] is None else acc_r[a] + pr
                            acc_i[a] = pi if acc_i[a] is None else acc_i[a] + pi
                for a in range(SUB):
                    zb[0, tile, hi * SUB + a] = acc_r[a]
                    zb[1, tile, hi * SUB + a] = acc_i[a]
            return 0

        lax.fori_loop(0, 2, combine, 0)
        whole = jnp.concatenate(
            [zb[p, t].reshape(nc * SUB, LANES) for p in range(2) for t in range(2)], axis=1
        )
        yb[g] = dot3(whole, ih[...], il[...]).reshape(nc, SUB, block)
        cb[g, c] = yb[g, c]
        for t in others:
            to_place(g, t).start()

    def receive(g):
        all_place(g).wait_recv()
        for j in range(gwide // LANES):
            rows = cb[g, j * per:(j + 1) * per].reshape(LANES, block)
            cols = slice(g * gwide + j * LANES, g * gwide + (j + 1) * LANES)
            signal = k[:, cols].astype(F32) * v[:, cols].astype(F32)
            gate = q[:, cols].astype(F32) * (rows.T + dr[:, cols] * signal)
            gate = gate.astype(BF16)
            gated[:, cols] = gate
            gate = gate.astype(F32).reshape(2, PARTS, rows_of, LANES)
            gown[:, g, :, :, j * LANES:(j + 1) * LANES] = gate
        for part in range(PARTS):
            for way in range(2):
                gated_hop(way, g, part).start()

    def local(g, way, s):
        dest = lax.rem(z + (nz - 1 - s if way == 0 else 1 + s), nz)
        cols = pl.ds(pl.multiple_of(dest * out_cols, out_cols), out_cols)
        terms = jnp.dot(
            gated[way * half:(way + 1) * half, g * gwide:(g + 1) * gwide],
            w[g * gwide:(g + 1) * gwide, cols],
            preferred_element_type=F32,
        ).reshape(PARTS, rows_of, out_cols)
        snd[way, s] = terms if g == 0 else snd[way, s] + terms

    convolve(0)
    convolve(1)
    for way in range(2):
        to_next(way).wait_recv()
    to_sibling().start()
    loads[-1].wait()
    receive(0)

    def fill(s, _):
        for way in range(2):
            local(0, way, s)
        return 0

    lax.fori_loop(1, nz, fill, 0)
    to_sibling().wait_recv()
    wnext[...] = wfar[...].astype(BF16)
    for way in range(2):
        for part in range(PARTS):
            gated_hop(way, 0, part).wait_recv()
            snd[way, 1, part] = snd[way, 1, part] + jnp.dot(
                gfar[way, 0, part].astype(BF16), wnext[way, :gwide], preferred_element_type=F32
            )
    receive(1)
    for way in range(2):
        local(1, way, 1)
    for part in range(PARTS):
        for way in range(2):
            gated_hop(way, 1, part).wait_recv()
            snd[way, 1, part] = snd[way, 1, part] + jnp.dot(
                gfar[way, 1, part].astype(BF16), wnext[way, gwide:], preferred_element_type=F32
            )
            hop(way, part, 1).start()

    def ring(s, _):
        for way in range(2):
            local(1, way, s)
        for part in range(PARTS):
            for way in range(2):
                hop(way, part, s - 1).wait_recv()
                snd[way, s, part] = snd[way, s, part] + rcv[way, s - 1, part]
                hop(way, part, s).start()
        return 0

    lax.fori_loop(2, nz - 1, ring, 0)
    for way in range(2):
        local(1, way, nz - 1)
    for part in range(PARTS):
        for way in range(2):
            hop(way, part, nz - 2).wait_recv()
            at = way * half + part * rows_of
            o_ref[at:at + rows_of] = (snd[way, nz - 1, part] + rcv[way, nz - 2, part]).astype(BF16)

    all_owner(1).wait_send()
    for g in range(groups):
        all_place(g).wait_send()
    all_hops().wait_send()
    all_gated().wait_send()
    for way in range(2):
        to_next(way).wait_send()
    to_sibling().wait_send()


def solution(mesh):
    nc, nz = mesh.shape["ctx"], mesh.shape["tp"]

    def body(query, keys, values, filt, direct, w_out):
        block, chans = keys.shape
        out_cols = w_out.shape[1] // nz
        groups = chans // nc // SUB
        gwide = chans // groups
        consts = [jnp.asarray(t) for t in tables(block)]
        operands = [query, keys, values, filt, direct.reshape(1, chans)] + consts + [w_out]
        rows_of = block // 2 // PARTS
        copies = [pltpu.VMEM(x.shape, x.dtype) for x in operands]
        dma = pltpu.SemaphoreType.DMA
        operands = [pltpu.with_memory_space_constraint(x, pltpu.HBM) for x in operands]
        return pl.pallas_call(
            functools.partial(kernel, nc, nz),
            out_shape=jax.ShapeDtypeStruct((block, out_cols), BF16),
            in_specs=[pl.BlockSpec(memory_space=pltpu.HBM)] * len(operands),
            out_specs=pl.BlockSpec(memory_space=pltpu.VMEM),
            scratch_shapes=copies
            + [
                pltpu.VMEM((groups, 2, nc, SUB, block), F32),
                pltpu.VMEM((groups, 2, nc, SUB, block), F32),
                pltpu.VMEM((2, 2, nc, SUB, LANES), F32),
                pltpu.VMEM((2, 2, nc + SUB, SUB, LANES), F32),
                pltpu.VMEM((2, 2, nc, SUB, LANES), F32),
                pltpu.VMEM((groups, nc, SUB, block), F32),
                pltpu.VMEM((groups, nc, SUB, block), F32),
                pltpu.VMEM((block, chans), BF16),
                pltpu.VMEM((2, nz, PARTS, rows_of, out_cols), F32),
                pltpu.VMEM((2, nz - 1, PARTS, rows_of, out_cols), F32),
                pltpu.VMEM((2, gwide, out_cols), BF16),
                pltpu.VMEM((2, gwide, out_cols), F32),
                pltpu.VMEM((2, chans, out_cols), F32),
                pltpu.VMEM((2, chans, out_cols), BF16),
                pltpu.VMEM((2, groups, PARTS, rows_of, gwide), F32),
                pltpu.VMEM((2, groups, PARTS, rows_of, gwide), F32),
                dma((len(operands) + 2,)),
                dma((groups,)),
                dma((groups,)),
                dma((groups,)),
                dma((groups,)),
                dma((1,)),
                dma((2, nz - 2, PARTS)),
                dma((3,)),
                dma((3,)),
                dma((1,)),
                dma((2, groups, PARTS)),
            ],
            compiler_params=pltpu.CompilerParams(
                collective_id=0, has_side_effects=True, vmem_limit_bytes=48 * 2**20
            ),
        )(*operands)

    return jax.shard_map(
        body,
        mesh=mesh,
        in_specs=(
            P("ctx", "tp"),
            P("ctx", "tp"),
            P("ctx", "tp"),
            P("ctx", "tp"),
            P("tp"),
            P("tp", None),
        ),
        out_specs=P("ctx", "tp"),
        check_vma=False,
    )
```

```python
import functools
import math

import jax
import jax.numpy as jnp
import numpy as np
from jax import lax
from jax.experimental import pallas as pl
from jax.experimental.pallas import tpu as pltpu
from jax.sharding import PartitionSpec as P

MESH = pl.DeviceIdType.MESH
F32 = jnp.float32
BF16 = jnp.bfloat16
LANES = 128
SUB = 8
PARTS = 4
SIDE = 4
NEAR = (0, 1, 2, -1)
STEPS = sorted(
    ((dx, dy, dk) for dx in NEAR for dy in NEAR for dk in (0, 1)),
    key=lambda n: (abs(n[0]) + abs(n[1]), n[2]),
)[:0:-1]


def tables(block):
    order = np.concatenate([np.arange(0, block, 2), np.arange(1, block, 2)])
    place = np.arange(block)
    angle = math.pi * (2 * order[None, :] + 1) * place[:, None] / (2 * block)
    forward = np.concatenate([np.cos(angle), -np.sin(angle)], axis=1)
    inverse = np.concatenate([np.cos(angle.T), -np.sin(angle.T)], axis=0) / block
    out = []
    for table in (forward, inverse):
        high = table.astype(jnp.bfloat16)
        low = (table - high.astype(np.float64)).astype(jnp.bfloat16)
        out += [high, low]
    return out


def split(x):
    high = x.astype(BF16)
    return high, (x - high.astype(F32)).astype(BF16)


def dot3(x, high, low):
    xh, xl = split(x)
    total = jnp.dot(xh, low, preferred_element_type=F32)
    total += jnp.dot(xl, high, preferred_element_type=F32)
    return total + jnp.dot(xh, high, preferred_element_type=F32)


def kernel(
    nc, nz,
    q_hbm, k_hbm, v_hbm, f_hbm, d_hbm, th_hbm, tl_hbm, ih_hbm, il_hbm, w_hbm,
    o_ref,
    q, k, v, f, dr, th, tl, ih, il, w,
    sbuf, rbuf, sb, gb, zb, yb, cb, gated, snd, rcv, wpart, wown, wfar, wnext, gown, gfar,
    lsem, asend, arecv, bsend, brecv, zsend, zrecv, wsend, wrecv, gsend, grecv,
):
    c = lax.axis_index("ctx")
    z = lax.axis_index("tp")
    block, chans = k.shape
    groups = sbuf.shape[0]
    gwide = chans // groups
    out_cols = o_ref.shape[1]
    half = block // 2
    rows_of = half // PARTS

    core, px, py = lax.rem(c, 2), lax.rem(c // 2, SIDE), c // (2 * SIDE)

    barrier = pltpu.get_barrier_semaphore()

    def partner(n):
        dx, dy, dk = STEPS[n]
        x, y = lax.rem(px + dx + SIDE, SIDE), lax.rem(py + dy + SIDE, SIDE)
        return (y * SIDE + x) * 2 + lax.rem(core + dk, 2)

    others = [partner(n) for n in range(nc - 1)]
    for t in others:
        pl.semaphore_signal(barrier, inc=1, device_id=(t, z), device_id_type=MESH)
    right, left = lax.rem(z + 1, nz), lax.rem(z + nz - 1, nz)
    for other in (right, left):
        pl.semaphore_signal(barrier, inc=1, device_id=(c, other), device_id_type=MESH)

    sibling = c + 1 - 2 * core
    wrows = pl.ds(pl.multiple_of(core * gwide, gwide), gwide)

    def block_of(step):
        at = lax.rem(z + nz + step, nz) * out_cols
        return pl.ds(pl.multiple_of(at, out_cols), out_cols)

    loads = [
        pltpu.make_async_copy(src, dst, lsem.at[n])
        for n, (src, dst) in enumerate(
            [(k_hbm, k), (v_hbm, v), (f_hbm, f), (q_hbm, q), (d_hbm, dr),
             (th_hbm, th), (tl_hbm, tl), (ih_hbm, ih), (il_hbm, il), (w_hbm, w)]
        )
    ]
    first = [
        pltpu.make_async_copy(
            w_hbm.at[wrows, block_of(1 if way else -1)], wpart.at[way], lsem.at[len(loads) + way]
        )
        for way in range(2)
    ]
    for load in loads[:3] + first:
        load.start()

    loads[0].wait()
    loads[1].wait()
    loads[2].wait()
    per = LANES // SUB
    for j in range(chans // LANES):
        cols = slice(j * LANES, (j + 1) * LANES)
        g, at = divmod(j * LANES, gwide)
        at = at // SUB
        for which in range(2):
            if which == 0:
                part = k[:, cols].astype(F32) * v[:, cols].astype(F32)
            else:
                part = f[:, cols]
            sbuf[g, which, at:at + per] = part.T.reshape(per, SUB, block)
    for g in range(groups):
        rbuf[g, :, c] = sbuf[g, :, c]
    for way in range(2):
        first[way].wait()
        wown[way] = wpart[way].astype(F32)
    pl.semaphore_wait(barrier, nc + 1)

    def to_owner(g, t):
        return pltpu.make_async_remote_copy(
            sbuf.at[g, :, t], rbuf.at[g, :, c], asend.at[g], arecv.at[g],
            device_id=(t, z), device_id_type=MESH,
        )

    def to_place(g, t):
        return pltpu.make_async_remote_copy(
            yb.at[g, t], cb.at[g, c], bsend.at[g], brecv.at[g],
            device_id=(t, z), device_id_type=MESH,
        )

    def all_owner(g):
        blocks = pl.ds(0, nc - 1)
        return pltpu.make_async_remote_copy(
            sbuf.at[g, :, blocks], rbuf.at[g, :, blocks], asend.at[g], arecv.at[g],
            device_id=(others[0], z), device_id_type=MESH,
        )

    def all_place(g):
        blocks = pl.ds(0, nc - 1)
        return pltpu.make_async_remote_copy(
            yb.at[g, blocks], cb.at[g, blocks], bsend.at[g], brecv.at[g],
            device_id=(others[0], z), device_id_type=MESH,
        )

    def all_hops():
        steps = pl.ds(1, nz - 2)
        return pltpu.make_async_remote_copy(
            snd.at[:, steps], rcv.at[:, steps], zsend.at[0], zrecv.at[0, 0, 0],
            device_id=(c, right), device_id_type=MESH,
        )

    def hop(way, part, s):
        return pltpu.make_async_remote_copy(
            snd.at[way, s, part], rcv.at[way, s, part],
            zsend.at[0], zrecv.at[way, s - 1, part],
            device_id=(c, right if way == 0 else left), device_id_type=MESH,
        )

    def to_next(way):
        return pltpu.make_async_remote_copy(
            wown.at[way], wfar.at[way, wrows], wsend.at[way], wrecv.at[way],
            device_id=(c, right if way == 0 else left), device_id_type=MESH,
        )

    def to_sibling():
        rows = wfar.at[:, wrows]
        return pltpu.make_async_remote_copy(
            rows, rows, wsend.at[2], wrecv.at[2], device_id=(sibling, z), device_id_type=MESH
        )

    def gated_hop(way, g, part):
        return pltpu.make_async_remote_copy(
            gown.at[way, g, part], gfar.at[way, g, part],
            gsend.at[0], grecv.at[way, g, part],
            device_id=(c, right if way == 0 else left), device_id_type=MESH,
        )

    def all_gated():
        return pltpu.make_async_remote_copy(
            gown, gfar, gsend.at[0], grecv.at[0, 0, 0],
            device_id=(c, right), device_id_type=MESH,
        )

    for t in others:
        to_owner(0, t).start()
    for way in range(2):
        to_next(way).start()
    for load in loads[3:]:
        load.start()
    for load in loads[3:-1]:
        load.wait()
    all_owner(0).wait_send()
    for t in others:
        to_owner(1, t).start()

    gb[:, :, 0:SUB] = jnp.zeros((2, 2, SUB, SUB, LANES), F32)

    def convolve(g):
        all_owner(g).wait_recv()
        flat = (nc * SUB, block)
        spec = dot3(rbuf[g, 0].reshape(flat), th[...], tl[...])
        for part in range(2):
            for tile in range(2):
                at = part * block + tile * half
                sb[tile, part] = spec[:, at:at + half].reshape(nc, SUB, LANES)
        spec = dot3(rbuf[g, 1].reshape(flat), th[...], tl[...])
        zero = jnp.zeros((1, SUB, LANES), F32)
        for tile in range(2):
            at = tile * half
            real = spec[:, at:at + half].reshape(nc, SUB, LANES)
            imag = spec[:, block + at:block + at + half].reshape(nc, SUB, LANES)
            real_b = jnp.concatenate([zero, real[:-1]], axis=0)
            imag_b = jnp.concatenate([zero, imag[:-1]], axis=0)
            if tile == 0:
                real, imag = real - imag_b, imag + real_b
            else:
                real, imag = real + imag_b, imag - real_b
            gb[tile, 0, SUB:] = real
            gb[tile, 1, SUB:] = imag

        def combine(tile, _):
            for hi in range(nc // SUB):
                acc = [[None] * SUB for _ in range(3)]
                for lo in range(hi + 1):
                    srcs = []
                    for n in range(SUB):
                        sr, si = sb[tile, 0, lo * SUB + n], sb[tile, 1, lo * SUB + n]
                        srcs.append((sr + si, sr, si))
                    base = (hi - lo) * SUB
                    for diff in range(1 - SUB, SUB):
                        if base + diff < 0:
                            continue
                        fr = gb[tile, 0, SUB + base + diff]
                        fi = gb[tile, 1, SUB + base + diff]
                        terms = (fr, fi - fr, fr + fi)
                        for n in range(SUB):
                            a = n + diff
                            if a < 0 or a >= SUB:
                                continue
                            for m in range(3):
                                prod = srcs[n][m] * terms[m]
                                acc[m][a] = prod if acc[m][a] is None else acc[m][a] + prod
                for a in range(SUB):
                    zb[0, tile, hi * SUB + a] = acc[0][a] - acc[2][a]
                    zb[1, tile, hi * SUB + a] = acc[0][a] + acc[1][a]
            return 0

        lax.fori_loop(0, 2, combine, 0)
        whole = jnp.concatenate(
            [zb[p, t].reshape(nc * SUB, LANES) for p in range(2) for t in range(2)], axis=1
        )
        yb[g] = dot3(whole, ih[...], il[...]).reshape(nc, SUB, block)
        cb[g, c] = yb[g, c]
        for t in others:
            to_place(g, t).start()

    def receive(g):
        all_place(g).wait_recv()
        for j in range(gwide // LANES):
            rows = cb[g, j * per:(j + 1) * per].reshape(LANES, block)
            cols = slice(g * gwide + j * LANES, g * gwide + (j + 1) * LANES)
            signal = k[:, cols].astype(F32) * v[:, cols].astype(F32)
            gate = q[:, cols].astype(F32) * (rows.T + dr[:, cols] * signal)
            gate = gate.astype(BF16)
            gated[:, cols] = gate
            gate = gate.astype(F32).reshape(2, PARTS, rows_of, LANES)
            gown[:, g, :, :, j * LANES:(j + 1) * LANES] = gate
        for part in range(PARTS):
            for way in range(2):
                gated_hop(way, g, part).start()

    def local(g, way, s):
        dest = lax.rem(z + (nz - 1 - s if way == 0 else 1 + s), nz)
        cols = pl.ds(pl.multiple_of(dest * out_cols, out_cols), out_cols)
        terms = jnp.dot(
            gated[way * half:(way + 1) * half, g * gwide:(g + 1) * gwide],
            w[g * gwide:(g + 1) * gwide, cols],
            preferred_element_type=F32,
        ).reshape(PARTS, rows_of, out_cols)
        snd[way, s] = terms if g == 0 else snd[way, s] + terms

    convolve(0)
    convolve(1)
    for way in range(2):
        to_next(way).wait_recv()
    to_sibling().start()
    loads[-1].wait()
    receive(0)

    def fill(s, _):
        for way in range(2):
            local(0, way, s)
        return 0

    lax.fori_loop(1, nz, fill, 0)
    to_sibling().wait_recv()
    wnext[...] = wfar[...].astype(BF16)
    for way in range(2):
        for part in range(PARTS):
            gated_hop(way, 0, part).wait_recv()
            snd[way, 1, part] = snd[way, 1, part] + jnp.dot(
                gfar[way, 0, part].astype(BF16), wnext[way, :gwide], preferred_element_type=F32
            )
    receive(1)
    for way in range(2):
        local(1, way, 1)
    for part in range(PARTS):
        for way in range(2):
            gated_hop(way, 1, part).wait_recv()
            snd[way, 1, part] = snd[way, 1, part] + jnp.dot(
                gfar[way, 1, part].astype(BF16), wnext[way, gwide:], preferred_element_type=F32
            )
            hop(way, part, 1).start()

    def ring(s, _):
        for way in range(2):
            local(1, way, s)
        for part in range(PARTS):
            for way in range(2):
                hop(way, part, s - 1).wait_recv()
                snd[way, s, part] = snd[way, s, part] + rcv[way, s - 1, part]
                hop(way, part, s).start()
        return 0

    lax.fori_loop(2, nz - 1, ring, 0)
    for way in range(2):
        local(1, way, nz - 1)
    for part in range(PARTS):
        for way in range(2):
            hop(way, part, nz - 2).wait_recv()
            at = way * half + part * rows_of
            o_ref[at:at + rows_of] = (snd[way, nz - 1, part] + rcv[way, nz - 2, part]).astype(BF16)

    all_owner(1).wait_send()
    for g in range(groups):
        all_place(g).wait_send()
    all_hops().wait_send()
    all_gated().wait_send()
    for way in range(2):
        to_next(way).wait_send()
    to_sibling().wait_send()


def solution(mesh):
    nc, nz = mesh.shape["ctx"], mesh.shape["tp"]

    def body(query, keys, values, filt, direct, w_out):
        block, chans = keys.shape
        out_cols = w_out.shape[1] // nz
        groups = chans // nc // SUB
        gwide = chans // groups
        consts = [jnp.asarray(t) for t in tables(block)]
        operands = [query, keys, values, filt, direct.reshape(1, chans)] + consts + [w_out]
        rows_of = block // 2 // PARTS
        copies = [pltpu.VMEM(x.shape, x.dtype) for x in operands]
        dma = pltpu.SemaphoreType.DMA
        operands = [pltpu.with_memory_space_constraint(x, pltpu.HBM) for x in operands]
        return pl.pallas_call(
            functools.partial(kernel, nc, nz),
            out_shape=jax.ShapeDtypeStruct((block, out_cols), BF16),
            in_specs=[pl.BlockSpec(memory_space=pltpu.HBM)] * len(operands),
            out_specs=pl.BlockSpec(memory_space=pltpu.VMEM),
            scratch_shapes=copies
            + [
                pltpu.VMEM((groups, 2, nc, SUB, block), F32),
                pltpu.VMEM((groups, 2, nc, SUB, block), F32),
                pltpu.VMEM((2, 2, nc, SUB, LANES), F32),
                pltpu.VMEM((2, 2, nc + SUB, SUB, LANES), F32),
                pltpu.VMEM((2, 2, nc, SUB, LANES), F32),
                pltpu.VMEM((groups, nc, SUB, block), F32),
                pltpu.VMEM((groups, nc, SUB, block), F32),
                pltpu.VMEM((block, chans), BF16),
                pltpu.VMEM((2, nz, PARTS, rows_of, out_cols), F32),
                pltpu.VMEM((2, nz - 1, PARTS, rows_of, out_cols), F32),
                pltpu.VMEM((2, gwide, out_cols), BF16),
                pltpu.VMEM((2, gwide, out_cols), F32),
                pltpu.VMEM((2, chans, out_cols), F32),
                pltpu.VMEM((2, chans, out_cols), BF16),
                pltpu.VMEM((2, groups, PARTS, rows_of, gwide), F32),
                pltpu.VMEM((2, groups, PARTS, rows_of, gwide), F32),
                dma((len(operands) + 2,)),
                dma((groups,)),
                dma((groups,)),
                dma((groups,)),
                dma((groups,)),
                dma((1,)),
                dma((2, nz - 2, PARTS)),
                dma((3,)),
                dma((3,)),
                dma((1,)),
                dma((2, groups, PARTS)),
            ],
            compiler_params=pltpu.CompilerParams(
                collective_id=0, has_side_effects=True, vmem_limit_bytes=48 * 2**20
            ),
        )(*operands)

    return jax.shard_map(
        body,
        mesh=mesh,
        in_specs=(
            P("ctx", "tp"),
            P("ctx", "tp"),
            P("ctx", "tp"),
            P("ctx", "tp"),
            P("tp"),
            P("tp", None),
        ),
        out_specs=P("ctx", "tp"),
        check_vma=False,
    )
```

```python
import functools
import math

import jax
import jax.numpy as jnp
import numpy as np
from jax import lax
from jax.experimental import pallas as pl
from jax.experimental.pallas import tpu as pltpu
from jax.sharding import PartitionSpec as P

MESH = pl.DeviceIdType.MESH
F32 = jnp.float32
BF16 = jnp.bfloat16
LANES = 128
SUB = 8
PARTS = 4
SIDE = 4
NEAR = (0, 1, 2, -1)
STEPS = sorted(
    ((dx, dy, dk) for dx in NEAR for dy in NEAR for dk in (0, 1)),
    key=lambda n: (abs(n[0]) + abs(n[1]), n[2]),
)[:0:-1]


def tables(block):
    order = np.concatenate([np.arange(0, block, 2), np.arange(1, block, 2)])
    place = np.arange(block)
    angle = math.pi * (2 * order[None, :] + 1) * place[:, None] / (2 * block)
    forward = np.concatenate([np.cos(angle), -np.sin(angle)], axis=1)
    inverse = np.concatenate([np.cos(angle.T), -np.sin(angle.T)], axis=0) / block
    out = []
    for table in (forward, inverse):
        high = table.astype(jnp.bfloat16)
        low = (table - high.astype(np.float64)).astype(jnp.bfloat16)
        out += [high, low]
    return out


def split(x):
    high = x.astype(BF16)
    return high, (x - high.astype(F32)).astype(BF16)


def dot3(x, high, low):
    xh, xl = split(x)
    total = jnp.dot(xh, low, preferred_element_type=F32)
    total += jnp.dot(xl, high, preferred_element_type=F32)
    return total + jnp.dot(xh, high, preferred_element_type=F32)


def kernel(
    nc, nz,
    q_hbm, k_hbm, v_hbm, f_hbm, d_hbm, th_hbm, tl_hbm, ih_hbm, il_hbm, w_hbm,
    o_ref,
    q, k, v, f, dr, th, tl, ih, il, w,
    sbuf, rbuf, sb, gb, zb, yb, cb, gated, snd, rcv, wpart, wown, wfar, wnext, gown, gfar,
    lsem, asend, arecv, bsend, brecv, zsend, zrecv, wsend, wrecv, gsend, grecv,
):
    c = lax.axis_index("ctx")
    z = lax.axis_index("tp")
    block, chans = k.shape
    groups = sbuf.shape[0]
    gwide = chans // groups
    out_cols = o_ref.shape[1]
    half = block // 2
    rows_of = half // PARTS

    core, px, py = lax.rem(c, 2), lax.rem(c // 2, SIDE), c // (2 * SIDE)

    barrier = pltpu.get_barrier_semaphore()

    def partner(n):
        dx, dy, dk = STEPS[n]
        x, y = lax.rem(px + dx + SIDE, SIDE), lax.rem(py + dy + SIDE, SIDE)
        return (y * SIDE + x) * 2 + lax.rem(core + dk, 2)

    others = [partner(n) for n in range(nc - 1)]
    for t in others:
        pl.semaphore_signal(barrier, inc=1, device_id=(t, z), device_id_type=MESH)
    right, left = lax.rem(z + 1, nz), lax.rem(z + nz - 1, nz)
    for other in (right, left):
        pl.semaphore_signal(barrier, inc=1, device_id=(c, other), device_id_type=MESH)

    sibling = c + 1 - 2 * core
    wrows = pl.ds(pl.multiple_of(core * gwide, gwide), gwide)

    def block_of(step):
        at = lax.rem(z + nz + step, nz) * out_cols
        return pl.ds(pl.multiple_of(at, out_cols), out_cols)

    loads = [
        pltpu.make_async_copy(src, dst, lsem.at[n])
        for n, (src, dst) in enumerate(
            [(k_hbm, k), (v_hbm, v), (f_hbm, f), (q_hbm, q), (d_hbm, dr),
             (th_hbm, th), (tl_hbm, tl), (ih_hbm, ih), (il_hbm, il), (w_hbm, w)]
        )
    ]
    first = [
        pltpu.make_async_copy(
            w_hbm.at[wrows, block_of(1 if way else -1)], wpart.at[way], lsem.at[len(loads) + way]
        )
        for way in range(2)
    ]
    for load in loads[:3] + first:
        load.start()

    loads[0].wait()
    loads[1].wait()
    loads[2].wait()
    per = LANES // SUB
    for j in range(chans // LANES):
        cols = slice(j * LANES, (j + 1) * LANES)
        g, at = divmod(j * LANES, gwide)
        at = at // SUB
        for which in range(2):
            if which == 0:
                part = k[:, cols].astype(F32) * v[:, cols].astype(F32)
            else:
                part = f[:, cols]
            sbuf[g, which, at:at + per] = part.T.reshape(per, SUB, block)
    for g in range(groups):
        rbuf[g, :, c] = sbuf[g, :, c]
    for way in range(2):
        first[way].wait()
        wown[way] = wpart[way].astype(F32)
    pl.semaphore_wait(barrier, nc + 1)

    def to_owner(g, t):
        return pltpu.make_async_remote_copy(
            sbuf.at[g, :, t], rbuf.at[g, :, c], asend.at[g], arecv.at[g],
            device_id=(t, z), device_id_type=MESH,
        )

    def to_place(g, t):
        return pltpu.make_async_remote_copy(
            yb.at[g, t], cb.at[g, c], bsend.at[g], brecv.at[g],
            device_id=(t, z), device_id_type=MESH,
        )

    def all_owner(g):
        blocks = pl.ds(0, nc - 1)
        return pltpu.make_async_remote_copy(
            sbuf.at[g, :, blocks], rbuf.at[g, :, blocks], asend.at[g], arecv.at[g],
            device_id=(others[0], z), device_id_type=MESH,
        )

    def all_place(g):
        blocks = pl.ds(0, nc - 1)
        return pltpu.make_async_remote_copy(
            yb.at[g, blocks], cb.at[g, blocks], bsend.at[g], brecv.at[g],
            device_id=(others[0], z), device_id_type=MESH,
        )

    def all_hops():
        steps = pl.ds(1, nz - 2)
        return pltpu.make_async_remote_copy(
            snd.at[:, steps], rcv.at[:, steps], zsend.at[0], zrecv.at[0, 0, 0],
            device_id=(c, right), device_id_type=MESH,
        )

    def hop(way, part, s):
        return pltpu.make_async_remote_copy(
            snd.at[way, s, part], rcv.at[way, s, part],
            zsend.at[0], zrecv.at[way, s - 1, part],
            device_id=(c, right if way == 0 else left), device_id_type=MESH,
        )

    def to_next(way):
        return pltpu.make_async_remote_copy(
            wown.at[way], wfar.at[way, wrows], wsend.at[way], wrecv.at[way],
            device_id=(c, right if way == 0 else left), device_id_type=MESH,
        )

    def to_sibling():
        rows = wfar.at[:, wrows]
        return pltpu.make_async_remote_copy(
            rows, rows, wsend.at[2], wrecv.at[2], device_id=(sibling, z), device_id_type=MESH
        )

    def gated_hop(way, g, part):
        return pltpu.make_async_remote_copy(
            gown.at[way, g, part], gfar.at[way, g, part],
            gsend.at[0], grecv.at[way, g, part],
            device_id=(c, right if way == 0 else left), device_id_type=MESH,
        )

    def all_gated():
        return pltpu.make_async_remote_copy(
            gown, gfar, gsend.at[0], grecv.at[0, 0, 0],
            device_id=(c, right), device_id_type=MESH,
        )

    for t in others:
        to_owner(0, t).start()
    for way in range(2):
        to_next(way).start()
    for load in loads[3:]:
        load.start()
    for load in loads[3:-1]:
        load.wait()
    all_owner(0).wait_send()
    for t in others:
        to_owner(1, t).start()

    gb[:, :, 0:SUB] = jnp.zeros((2, 2, SUB, SUB, LANES), F32)

    def convolve(g):
        all_owner(g).wait_recv()
        flat = (nc * SUB, block)
        spec = dot3(rbuf[g, 0].reshape(flat), th[...], tl[...])
        for part in range(2):
            for tile in range(2):
                at = part * block + tile * half
                sb[tile, part] = spec[:, at:at + half].reshape(nc, SUB, LANES)
        spec = dot3(rbuf[g, 1].reshape(flat), th[...], tl[...])
        zero = jnp.zeros((1, SUB, LANES), F32)
        for tile in range(2):
            at = tile * half
            real = spec[:, at:at + half].reshape(nc, SUB, LANES)
            imag = spec[:, block + at:block + at + half].reshape(nc, SUB, LANES)
            real_b = jnp.concatenate([zero, real[:-1]], axis=0)
            imag_b = jnp.concatenate([zero, imag[:-1]], axis=0)
            if tile == 0:
                real, imag = real - imag_b, imag + real_b
            else:
                real, imag = real + imag_b, imag - real_b
            gb[tile, 0, SUB:] = real
            gb[tile, 1, SUB:] = imag

        def combine(tile, _):
            for hi in range(nc // SUB):
                acc = [[None] * SUB for _ in range(3)]
                for lo in range(hi + 1):
                    srcs = []
                    for n in range(SUB):
                        sr, si = sb[tile, 0, lo * SUB + n], sb[tile, 1, lo * SUB + n]
                        srcs.append((sr + si, sr, si))
                    base = (hi - lo) * SUB
                    for diff in range(1 - SUB, SUB):
                        if base + diff < 0:
                            continue
                        fr = gb[tile, 0, SUB + base + diff]
                        fi = gb[tile, 1, SUB + base + diff]
                        terms = (fr, fi - fr, fr + fi)
                        for n in range(SUB):
                            a = n + diff
                            if a < 0 or a >= SUB:
                                continue
                            for m in range(3):
                                prod = srcs[n][m] * terms[m]
                                acc[m][a] = prod if acc[m][a] is None else acc[m][a] + prod
                for a in range(SUB):
                    zb[0, tile, hi * SUB + a] = acc[0][a] - acc[2][a]
                    zb[1, tile, hi * SUB + a] = acc[0][a] + acc[1][a]
            return 0

        combine(0, 0)
        combine(1, 0)
        whole = jnp.concatenate(
            [zb[p, t].reshape(nc * SUB, LANES) for p in range(2) for t in range(2)], axis=1
        )
        yb[g] = dot3(whole, ih[...], il[...]).reshape(nc, SUB, block)
        cb[g, c] = yb[g, c]
        for t in others:
            to_place(g, t).start()

    def receive(g):
        all_place(g).wait_recv()
        for j in range(gwide // LANES):
            rows = cb[g, j * per:(j + 1) * per].reshape(LANES, block)
            cols = slice(g * gwide + j * LANES, g * gwide + (j + 1) * LANES)
            signal = k[:, cols].astype(F32) * v[:, cols].astype(F32)
            gate = q[:, cols].astype(F32) * (rows.T + dr[:, cols] * signal)
            gate = gate.astype(BF16)
            gated[:, cols] = gate
            gate = gate.astype(F32).reshape(2, PARTS, rows_of, LANES)
            gown[:, g, :, :, j * LANES:(j + 1) * LANES] = gate
        for part in range(PARTS):
            for way in range(2):
                gated_hop(way, g, part).start()

    def local(g, way, s):
        dest = lax.rem(z + (nz - 1 - s if way == 0 else 1 + s), nz)
        cols = pl.ds(pl.multiple_of(dest * out_cols, out_cols), out_cols)
        terms = jnp.dot(
            gated[way * half:(way + 1) * half, g * gwide:(g + 1) * gwide],
            w[g * gwide:(g + 1) * gwide, cols],
            preferred_element_type=F32,
        ).reshape(PARTS, rows_of, out_cols)
        snd[way, s] = terms if g == 0 else snd[way, s] + terms

    convolve(0)
    convolve(1)
    for way in range(2):
        to_next(way).wait_recv()
    to_sibling().start()
    loads[-1].wait()
    receive(0)

    def fill(s, _):
        for way in range(2):
            local(0, way, s)
        return 0

    lax.fori_loop(1, nz, fill, 0)
    to_sibling().wait_recv()
    wnext[...] = wfar[...].astype(BF16)
    for way in range(2):
        for part in range(PARTS):
            gated_hop(way, 0, part).wait_recv()
            snd[way, 1, part] = snd[way, 1, part] + jnp.dot(
                gfar[way, 0, part].astype(BF16), wnext[way, :gwide], preferred_element_type=F32
            )
    receive(1)
    for way in range(2):
        local(1, way, 1)
    for part in range(PARTS):
        for way in range(2):
            gated_hop(way, 1, part).wait_recv()
            snd[way, 1, part] = snd[way, 1, part] + jnp.dot(
                gfar[way, 1, part].astype(BF16), wnext[way, gwide:], preferred_element_type=F32
            )
            hop(way, part, 1).start()

    def ring(s, _):
        for way in range(2):
            local(1, way, s)
        for part in range(PARTS):
            for way in range(2):
                hop(way, part, s - 1).wait_recv()
                snd[way, s, part] = snd[way, s, part] + rcv[way, s - 1, part]
                hop(way, part, s).start()
        return 0

    lax.fori_loop(2, nz - 1, ring, 0)
    for way in range(2):
        local(1, way, nz - 1)
    for part in range(PARTS):
        for way in range(2):
            hop(way, part, nz - 2).wait_recv()
            at = way * half + part * rows_of
            o_ref[at:at + rows_of] = (snd[way, nz - 1, part] + rcv[way, nz - 2, part]).astype(BF16)

    all_owner(1).wait_send()
    for g in range(groups):
        all_place(g).wait_send()
    all_hops().wait_send()
    all_gated().wait_send()
    for way in range(2):
        to_next(way).wait_send()
    to_sibling().wait_send()


def solution(mesh):
    nc, nz = mesh.shape["ctx"], mesh.shape["tp"]

    def body(query, keys, values, filt, direct, w_out):
        block, chans = keys.shape
        out_cols = w_out.shape[1] // nz
        groups = chans // nc // SUB
        gwide = chans // groups
        consts = [jnp.asarray(t) for t in tables(block)]
        operands = [query, keys, values, filt, direct.reshape(1, chans)] + consts + [w_out]
        rows_of = block // 2 // PARTS
        copies = [pltpu.VMEM(x.shape, x.dtype) for x in operands]
        dma = pltpu.SemaphoreType.DMA
        operands = [pltpu.with_memory_space_constraint(x, pltpu.HBM) for x in operands]
        return pl.pallas_call(
            functools.partial(kernel, nc, nz),
            out_shape=jax.ShapeDtypeStruct((block, out_cols), BF16),
            in_specs=[pl.BlockSpec(memory_space=pltpu.HBM)] * len(operands),
            out_specs=pl.BlockSpec(memory_space=pltpu.VMEM),
            scratch_shapes=copies
            + [
                pltpu.VMEM((groups, 2, nc, SUB, block), F32),
                pltpu.VMEM((groups, 2, nc, SUB, block), F32),
                pltpu.VMEM((2, 2, nc, SUB, LANES), F32),
                pltpu.VMEM((2, 2, nc + SUB, SUB, LANES), F32),
                pltpu.VMEM((2, 2, nc, SUB, LANES), F32),
                pltpu.VMEM((groups, nc, SUB, block), F32),
                pltpu.VMEM((groups, nc, SUB, block), F32),
                pltpu.VMEM((block, chans), BF16),
                pltpu.VMEM((2, nz, PARTS, rows_of, out_cols), F32),
                pltpu.VMEM((2, nz - 1, PARTS, rows_of, out_cols), F32),
                pltpu.VMEM((2, gwide, out_cols), BF16),
                pltpu.VMEM((2, gwide, out_cols), F32),
                pltpu.VMEM((2, chans, out_cols), F32),
                pltpu.VMEM((2, chans, out_cols), BF16),
                pltpu.VMEM((2, groups, PARTS, rows_of, gwide), F32),
                pltpu.VMEM((2, groups, PARTS, rows_of, gwide), F32),
                dma((len(operands) + 2,)),
                dma((groups,)),
                dma((groups,)),
                dma((groups,)),
                dma((groups,)),
                dma((1,)),
                dma((2, nz - 2, PARTS)),
                dma((3,)),
                dma((3,)),
                dma((1,)),
                dma((2, groups, PARTS)),
            ],
            compiler_params=pltpu.CompilerParams(
                collective_id=0, has_side_effects=True, vmem_limit_bytes=48 * 2**20
            ),
        )(*operands)

    return jax.shard_map(
        body,
        mesh=mesh,
        in_specs=(
            P("ctx", "tp"),
            P("ctx", "tp"),
            P("ctx", "tp"),
            P("ctx", "tp"),
            P("tp"),
            P("tp", None),
        ),
        out_specs=P("ctx", "tp"),
        check_vma=False,
    )
```
